128 devices in a mesh: fsdp: 4 (over x), table: 32 (over y, z, core).
Axes of the slice: x: 4, y: 4, z: 4, core: 2. Of those that a mesh axis runs over, the one named last changes fastest.
Arguments:
- embedded: bfloat16 [262144, 512], P(('fsdp', 'table')), may hold values from -6 to 6
- grad_out: bfloat16 [262144, 512], P(('fsdp', 'table')), may hold values from -6 to 6
- w_in: bfloat16 [512, 2048], P('fsdp'), may hold values from -0.25 to 0.25
- w_out: bfloat16 [512, 512], P('fsdp'), may hold values from -0.25 to 0.25
- lengths: int32 [512], P(('fsdp', 'table')), may hold values from 1 to 512, as said below
- slot_of: int32 [262144], P(('fsdp', 'table')), may hold values from 0 to 1613, as said below
- local_rows: int32 [206592], P(('fsdp', 'table')), may hold values from 0 to 4095, as said below
- send_counts: int32 [128, 32], P(('fsdp', 'table')), may hold values from 30 to 64, as said below
- send_offsets: int32 [128, 32], P(('fsdp', 'table')), may hold values from 0 to 1564, as said below
Outputs:
- grad_w_in: float32 [512, 2048], P('fsdp')
- grad_w_out: float32 [512, 512], P('fsdp')
- grad_table: float32 [131072, 512], P('table', 'fsdp')
The draws below stay inside these ranges and needn't reach their ends.
Inputs may be any that keep to these rules, and one draw needn't show every extreme that they name: `lengths`: at least one sequence has 512 real actions in every draw. `send_counts`: row d counts, for each owner o, the slots of device d whose items lie in rows o * 4096 to (o + 1) * 4096 - 1; in every draw one owner other than the last gets exactly 64 from every device, and some device sends exactly 50 to every other owner; a row sums to at most 1614. `send_offsets`: row d is the exclusive prefix sum of row d of send_counts, so each owner's slots are consecutive and in owner order. Action t of device d reads slot slot_of[t] of device d's list; the slots used are exactly those below the sum of row d of send_counts. `local_rows`: two used slots of one device and one owner hold different rows; slots past the used ones are ignored.
All inputs are finite; a program needn't handle non-finite values.
Results may differ from the reference program's by a relative error of at most 0.011.
Values may be sent and summed in bfloat16 or wider, within the bound.
No kernel may reach another device: no remote copies, remote signals or barrier semaphores. Data moves between devices by JAX's collectives and lax.ppermute only.
A program may use at most 256 MiB of HBM per device.

```python
import math
import jax
import jax.numpy as jnp
from jax import lax

D = 512
HEAD_DIM = 128
SEQ_LEN = 512
SEQ_DEV = 4
ROWS_DEV = 4096
CAP = 64
COUNT_HI = 50
TOK_DEV = 2048
UNIQ_DEV = 1614
TOKENS = 262144
TABLE_ROWS = 131072
N_FSDP = 4
N_TABLE = 32


def owner_loads(key):
    devices = N_FSDP * N_TABLE
    hot_owner = jax.random.randint(jax.random.fold_in(key, 101), (), 0, N_TABLE - 1)
    base_load = jax.random.randint(jax.random.fold_in(key, 102), (devices, N_TABLE), COUNT_HI * 3 // 5, COUNT_HI + 1)
    full_device = jax.random.randint(jax.random.fold_in(key, 103), (), 0, devices)
    device_ids = jnp.arange(devices)
    base_load = jnp.where(device_ids[:, None] == full_device, COUNT_HI, base_load)
    owner_ids = jnp.arange(N_TABLE)
    counts = jnp.where(owner_ids[None, :] == hot_owner, CAP, base_load).astype(jnp.int32)
    offsets = (jnp.cumsum(counts, axis=1) - counts).astype(jnp.int32)
    return (counts, offsets)


def draw_send_counts(key, part):
    counts, offsets = owner_loads(key)
    return counts


def draw_send_offsets(key, part):
    counts, offsets = owner_loads(key)
    return offsets


def draw_slot_of(key, part):
    counts, offsets = owner_loads(key)
    key = jax.random.fold_in(key, 3)
    devices = N_FSDP * N_TABLE
    used = jnp.sum(counts, axis=1).astype(jnp.int32)
    actions = jnp.arange(TOK_DEV, dtype=jnp.int32)
    extra = jax.random.randint(jax.random.fold_in(key, 1), (devices, TOK_DEV), 0, used[:, None])
    slots = jnp.where(actions[None, :] < used[:, None], actions[None, :], extra)
    scores = jax.random.randint(jax.random.fold_in(key, 2), (devices, TOK_DEV), 0, 65536) * TOK_DEV + actions[None, :]
    order = jnp.argsort(scores, axis=1)
    return jnp.take_along_axis(slots, order, axis=1).reshape(-1).astype(jnp.int32)


def draw_local_rows(key, part):
    counts, offsets = owner_loads(key)
    key = jax.random.fold_in(key, 5)
    devices = N_FSDP * N_TABLE
    row_ids = jnp.arange(ROWS_DEV, dtype=jnp.int32)
    scores = jax.random.randint(jax.random.fold_in(key, 1), (devices, N_TABLE, ROWS_DEV), 0, 4096) * ROWS_DEV + row_ids
    scores = jnp.where(row_ids == ROWS_DEV - 1, scores + 4096 * ROWS_DEV, scores)
    unused_vals, chosen = lax.top_k(scores, CAP)
    slot_pos = jnp.arange(UNIQ_DEV, dtype=jnp.int32)
    owner_ids = jnp.arange(N_TABLE, dtype=jnp.int32)
    owner_hit = (slot_pos[None, :, None] >= offsets[:, None, :]) & (slot_pos[None, :, None] < (offsets + counts)[:, None, :])
    owner = jnp.sum(jnp.where(owner_hit, owner_ids[None, None, :], 0), axis=2).astype(jnp.int32)
    place = jnp.clip(slot_pos[None, :] - jnp.take_along_axis(offsets, owner, axis=1), 0, CAP - 1)
    picked = jnp.take_along_axis(chosen.reshape(devices, N_TABLE * CAP), owner * CAP + place, axis=1)
    in_use = jnp.any(owner_hit, axis=2)
    spare = jax.random.randint(jax.random.fold_in(key, 2), (devices, UNIQ_DEV), 0, ROWS_DEV)
    return jnp.where(in_use, picked, spare).reshape(-1).astype(jnp.int32)


def draw_lengths(key, part):
    key = jax.random.fold_in(key, 7)
    seq_total = SEQ_DEV * N_FSDP * N_TABLE
    drawn = jax.random.randint(jax.random.fold_in(key, 1), (seq_total,), SEQ_LEN // 4, SEQ_LEN + 1)
    longest = jax.random.randint(jax.random.fold_in(key, 2), (), 0, seq_total)
    return jnp.where(jnp.arange(seq_total) == longest, SEQ_LEN, drawn).astype(jnp.int32)


def block_scale(stream_key, extent, cuts, low, high):
    def one(position, blocks):
        heights = jax.random.uniform(jax.random.fold_in(jax.random.fold_in(stream_key, 6), position), (blocks,), jnp.float32, low / len(cuts), high / len(cuts))
        return jnp.repeat(jnp.exp(heights), extent[position] // blocks).reshape((-1,) + (1,) * (len(extent) - position - 1))

    factor_of = one(*cuts[0])
    for cut in cuts[1:]:
        factor_of = factor_of * one(*cut)
    return factor_of


def noise(rng, dims, width, limit, pieces=(), kind=jnp.bfloat16):
    array = width * jax.random.normal(rng, dims, jnp.float32)
    if pieces:
        array = array * block_scale(rng, dims, pieces, -0.22, 0.18)
    return jnp.clip(array, -limit, limit).astype(kind)


def setup_inputs(seed: int = 0) -> dict:
    splits = jax.random.split(jax.random.key(seed), 10)
    return {
        "embedded": noise(splits[0], (TOKENS, D), 1.0, 6.0, ((0, 128),)),
        "grad_out": noise(splits[1], (TOKENS, D), 1.0, 6.0, ((0, 128),)),
        "w_in": noise(splits[2], (D, 4 * D), D ** -0.5, 0.25, ((0, 4),)),
        "w_out": noise(splits[3], (D, D), D ** -0.5, 0.25, ((0, 4),)),
        "lengths": draw_lengths(jax.random.fold_in(splits[9], 71), 0),
        "slot_of": draw_slot_of(jax.random.fold_in(splits[9], 71), 0),
        "local_rows": draw_local_rows(jax.random.fold_in(splits[9], 71), 0),
        "send_counts": draw_send_counts(jax.random.fold_in(splits[9], 71), 0),
        "send_offsets": draw_send_offsets(jax.random.fold_in(splits[9], 71), 0),
    }


def layer_norm(field):
    center = field - lax.optimization_barrier(jnp.mean(field, axis=-1, keepdims=True))
    spread = lax.optimization_barrier(jnp.mean(center * center, axis=-1, keepdims=True))
    return center * lax.rsqrt(spread + 1e-05)

def attend(hidden, seq_lens):
    seq_count = seq_lens.shape[0]
    model_width = hidden.shape[1] // 4
    seq_len = hidden.shape[0] // seq_count
    head_count = model_width // HEAD_DIM
    gating, values, queries, keys_in = jnp.split(hidden, 4, axis=1)

    def heads_of(block):
        return block.reshape(seq_count, seq_len, head_count, HEAD_DIM)
    positions = jnp.arange(seq_len, dtype=jnp.int32)
    causal = positions[None, :] <= positions[:, None]
    score_factor = 1.0 / math.sqrt(HEAD_DIM)

    def one_seq(items):
        query_seq, key_seq, value_seq, seq_length = items
        scores = jnp.einsum('qhd,khd->hqk', query_seq.astype(jnp.float32), key_seq.astype(jnp.float32)) * score_factor
        keep_mask = causal & (positions[:, None] < seq_length)
        weights_b = jnp.where(keep_mask[None], jax.nn.silu(scores) / seq_len, 0.0).astype(jnp.bfloat16)
        return jnp.einsum('hqk,khd->qhd', weights_b.astype(jnp.float32), value_seq.astype(jnp.float32))
    mixed = lax.map(one_seq, (heads_of(queries), heads_of(keys_in), heads_of(values), seq_lens))
    mixed = mixed.reshape(-1, model_width)
    return (layer_norm(mixed) * gating.astype(jnp.float32)).astype(jnp.bfloat16)

def layer_grads(embedded, grad_out, seq_lens, w_in, w_out):
    normed = layer_norm(embedded.astype(jnp.float32))
    normed_b = normed.astype(jnp.bfloat16)
    projected = jnp.dot(normed_b, w_in, preferred_element_type=jnp.float32)
    hidden = jax.nn.silu(projected).astype(jnp.bfloat16)
    mixed_b, attend_back = jax.vjp(lambda block: attend(block, seq_lens), hidden)
    grad_mixed = jnp.dot(grad_out, w_out.T, preferred_element_type=jnp.float32).astype(jnp.bfloat16)
    grad_wout = jnp.dot(mixed_b.T, grad_out, preferred_element_type=jnp.float32)
    grad_hidden, = attend_back(grad_mixed)
    sigma = jax.nn.sigmoid(projected)
    grad_proj = (grad_hidden.astype(jnp.float32) * sigma * (1.0 + projected * (1.0 - sigma))).astype(jnp.bfloat16)
    grad_win = jnp.dot(normed_b.T, grad_proj, preferred_element_type=jnp.float32)
    grad_normed = jnp.dot(grad_proj, w_in.T, preferred_element_type=jnp.float32)
    _, norm_back = jax.vjp(layer_norm, embedded.astype(jnp.float32))
    grad_embed, = norm_back(grad_normed)
    token_grad = (grad_embed + grad_out.astype(jnp.float32)).astype(jnp.bfloat16)
    return (token_grad, grad_win, grad_wout)

def reference(embedded, grad_out, w_in, w_out, lengths, slot_of, local_rows, send_counts, send_offsets):
    blocks = N_FSDP * N_TABLE
    embed_blocks = embedded.reshape(blocks, TOK_DEV, D)
    cotan_blocks = grad_out.reshape(blocks, TOK_DEV, D)
    length_blocks = lengths.reshape(blocks, SEQ_DEV)

    def step(carry, items):
        token_grad, grad_win, grad_wout = layer_grads(items[0], items[1], items[2], w_in, w_out)
        return ((carry[0] + grad_win, carry[1] + grad_wout), token_grad)
    start = (jnp.zeros((D, 4 * D), jnp.float32), jnp.zeros((D, D), jnp.float32))
    totals, token_grads = lax.scan(step, start, (embed_blocks, cotan_blocks, length_blocks))
    factor = 1.0 / math.sqrt(TOKENS)
    slot_pos = jnp.arange(UNIQ_DEV, dtype=jnp.int32)
    owner_ids = jnp.arange(N_TABLE, dtype=jnp.int32)
    lower = send_offsets[:, None, :]
    upper = (send_offsets + send_counts)[:, None, :]
    owner_hit = (slot_pos[None, :, None] >= lower) & (slot_pos[None, :, None] < upper)
    owner = lax.optimization_barrier(jnp.sum(jnp.where(owner_hit, owner_ids[None, None, :], 0), axis=2)).astype(jnp.int32)
    slot_items = (owner * ROWS_DEV + local_rows.reshape(blocks, UNIQ_DEV)).astype(jnp.int32)
    item_ids = jnp.take_along_axis(slot_items, slot_of.reshape(blocks, TOK_DEV), axis=1).reshape(-1).astype(jnp.int32)
    grad_table = jax.ops.segment_sum(token_grads.reshape(-1, D).astype(jnp.float32), item_ids, num_segments=TABLE_ROWS)
    return (totals[0] * factor, totals[1] * factor, grad_table)
```

```python
import functools
import math

import jax
import jax.numpy as jnp
from jax import lax
from jax.experimental import pallas as pl
from jax.experimental.pallas import tpu as pltpu
from jax.sharding import PartitionSpec as P

HEAD_DIM = 128
ROWS_DEV = 4096
CAP = 64
PACKET = 72
SEQ = 512
WIDTH = 512
HEADS = WIDTH // HEAD_DIM
HALF = SEQ // 2
EPS = 1e-05
BF = jnp.bfloat16
F32 = jnp.float32
BOTH = ("fsdp", "table")


def dot_nn(a, b):
    return lax.dot_general(a, b, (((1,), (0,)), ((), ())), preferred_element_type=F32)


def dot_nt(a, b):
    return lax.dot_general(a, b, (((1,), (1,)), ((), ())), preferred_element_type=F32)


def dot_tn(a, b):
    return lax.dot_general(a, b, (((0,), (0,)), ((), ())), preferred_element_type=F32)


def normalise(x):
    center = x - jnp.mean(x, axis=-1, keepdims=True)
    rstd = lax.rsqrt(jnp.mean(center * center, axis=-1, keepdims=True) + EPS)
    return center * rstd, rstd


def norm_back(xhat, rstd, cot):
    return rstd * (
        cot
        - jnp.mean(cot, axis=-1, keepdims=True)
        - xhat * jnp.mean(cot * xhat, axis=-1, keepdims=True)
    )


def norm_kernel(emb, after, normed, turned):
    chunk = 64

    @pl.loop(0, SEQ // chunk)
    def _(i):
        rows = pl.ds(pl.multiple_of(i * chunk, chunk), chunk)
        xhat, _ = normalise(emb[rows, :].astype(F32))
        normed[rows, :] = xhat.astype(BF)

    turned[...] = normed[...].T


def run_norm(embedded, after):
    tokens = embedded.shape[0]
    return pl.pallas_call(
        norm_kernel,
        grid=(tokens // SEQ,),
        in_specs=[
            pl.BlockSpec((SEQ, WIDTH), lambda i: (i, 0)),
            pl.BlockSpec(memory_space=pl.ANY),
        ],
        out_specs=[
            pl.BlockSpec((SEQ, WIDTH), lambda i: (i, 0)),
            pl.BlockSpec((WIDTH, SEQ), lambda i: (0, i)),
        ],
        out_shape=[
            jax.ShapeDtypeStruct((tokens, WIDTH), BF),
            jax.ShapeDtypeStruct((WIDTH, tokens), BF),
        ],
        compiler_params=pltpu.CompilerParams(vmem_limit_bytes=56 * 1024 * 1024),
        cost_estimate=pl.CostEstimate(
            flops=20_000_000, bytes_accessed=6_000_000, transcendentals=2048
        ),
        name="norm",
    )(embedded, after)


def layer_kernel(
    coords, lens, normed, go, turned, own_in, own_out,
    low, high, low_o, high_o, far_a, far_b, far_ao, far_bo,
    gp, mine, other, w_turned,
    w, proj, slope, hidden, probs, rates, mixed, cot, seq_sum, gp_all, gwout,
):
    step = pl.program_id(0)

    @pl.when(step == 0)
    def _():
        me, core = coords[0], coords[1]

        def put(shard, which, offset, piece):
            row = lax.rem(shard, 4) * 128 + which * 64 + offset
            w[pl.ds(pl.multiple_of(row, 32), piece.shape[0]), :] = piece[...]

        home = pl.ds(pl.multiple_of(me * 128, 128), 128)
        w[home, 0 : 4 * WIDTH] = own_in[...]
        w[home, 4 * WIDTH :] = own_out[...]
        put(me + 3, core, 0, low)
        put(me + 3, 1 - core, 0, low_o)
        put(me + 1, core, 0, high)
        put(me + 1, 1 - core, 0, high_o)
        put(me + 2, core, 0, far_a)
        put(me + 2, core, 32, far_b)
        put(me + 2, 1 - core, 0, far_ao)
        put(me + 2, 1 - core, 32, far_bo)
        gwout[...] = jnp.zeros_like(gwout)

        @pl.loop(0, 4)
        def _(i):
            cols = pl.ds(pl.multiple_of(i * WIDTH, WIDTH), WIDTH)
            w_turned[cols, :] = w[:, cols].T

    chunk = 64

    def rows_of(i, size=chunk):
        return pl.ds(pl.multiple_of(i * size, size), size)

    for block in range(4):
        cols = slice(block * WIDTH, (block + 1) * WIDTH)
        proj[...] = dot_nn(normed[...], w[:, cols])

        @pl.loop(0, SEQ // chunk)
        def _(i):
            half = 0.5 * proj[rows_of(i), :]
            t = jnp.tanh(half)
            ht = half * t
            hidden[rows_of(i), cols] = (half + ht).astype(BF)
            slope[rows_of(i), cols] = 0.5 * ((1.0 + half) + t * (1.0 - ht))

    factor = 0.5 / math.sqrt(HEAD_DIM)

    def head_cols(block, head):
        return slice(block * WIDTH + head * HEAD_DIM, block * WIDTH + (head + 1) * HEAD_DIM)

    causal = lax.broadcasted_iota(jnp.int32, (HALF, HALF), 1) <= lax.broadcasted_iota(
        jnp.int32, (HALF, HALF), 0
    )
    for head in range(HEADS):
        v_cols, q_cols, k_cols = (head_cols(b, head) for b in (1, 2, 3))
        for qi in range(2):
            q_rows = slice(qi * HALF, (qi + 1) * HALF)
            for ki in range(qi + 1):
                k_rows = slice(ki * HALF, (ki + 1) * HALF)
                z = factor * dot_nt(hidden[q_rows, q_cols], hidden[k_rows, k_cols])
                t = jnp.tanh(z)
                zt = z * t
                prob = z + zt
                rate = (1.0 + z) + t * (1.0 - zt)
                if qi == ki:
                    prob = jnp.where(causal, prob, 0.0)
                    rate = jnp.where(causal, rate, 0.0)
                probs[head, q_rows, k_rows] = prob.astype(BF)
                rates[head, q_rows, k_rows] = rate.astype(BF)
            seen = slice(0, (qi + 1) * HALF)
            mixed[q_rows, head_cols(0, head)] = dot_nn(
                probs[head, q_rows, seen], hidden[seen, v_cols]
            )

    proj[...] = dot_nt(go[...], w[:, 4 * WIDTH :])
    seq_len = lens[step]

    @pl.loop(0, SEQ // chunk)
    def _(i):
        rows = rows_of(i)
        place = lax.broadcasted_iota(jnp.int32, (chunk, 1), 0) + i * chunk
        keep = place < seq_len
        raw = jnp.where(keep, mixed[rows, :] * (1.0 / SEQ), 0.0)
        xhat, rstd = normalise(raw)
        gate = hidden[rows, 0:WIDTH].astype(F32)
        down = proj[rows, :].astype(BF).astype(F32)
        seq_sum[rows, :] = (xhat * gate).astype(BF)
        grad_gate = ((down * xhat).astype(BF).astype(F32) * slope[rows, 0:WIDTH]).astype(BF)
        gp[rows, 0:WIDTH] = grad_gate
        gp_all[pl.ds(pl.multiple_of(step * SEQ + i * chunk, chunk), chunk), 0:WIDTH] = grad_gate
        back = norm_back(xhat, rstd, down * gate)
        cot[rows, :] = jnp.where(keep, back * (1.0 / SEQ), 0.0).astype(BF)

    gwout[...] += dot_tn(seq_sum[...], go[...])

    def finish(value, rows, cols):
        grad = (value.astype(BF).astype(F32) * slope[rows, cols]).astype(BF)
        gp[rows, cols] = grad
        here = pl.ds(pl.multiple_of(step * SEQ + rows.start, HALF), rows.stop - rows.start)
        gp_all[here, cols] = grad

    top, low_half, whole = slice(0, HALF), slice(HALF, SEQ), slice(0, SEQ)
    for head in range(HEADS):
        v_cols, q_cols, k_cols = (head_cols(b, head) for b in (1, 2, 3))
        c_cols = head_cols(0, head)
        for q_rows, seen in ((top, top), (low_half, whole)):
            down = dot_nt(cot[q_rows, c_cols], hidden[seen, v_cols]).astype(BF)
            score = down * rates[head, q_rows, seen]
            rates[head, q_rows, seen] = score
            finish(factor * dot_nn(score, hidden[seen, k_cols]), q_rows, q_cols)
        for k_rows, seen in ((top, whole), (low_half, low_half)):
            finish(dot_tn(probs[head, seen, k_rows], cot[seen, c_cols]), k_rows, v_cols)
            finish(
                factor * dot_tn(rates[head, seen, k_rows], hidden[seen, q_cols]),
                k_rows,
                k_cols,
            )

    @pl.when(step == pl.num_programs(0) - 1)
    def _():
        tile, per_half = 256, 5
        core = coords[1]

        def place(half, col, value):
            cols = pl.ds(pl.multiple_of(col, tile), value.shape[1])

            @pl.when(half == core)
            def _():
                mine[:, cols] = value

            @pl.when(half != core)
            def _():
                other[:, cols] = value

        @pl.loop(0, 4 * WIDTH // tile)
        def _(j):
            cols = pl.ds(pl.multiple_of(j * tile, tile), tile)
            value = dot_nn(turned[...], gp_all[:, cols]).astype(BF)
            place(j // per_half, lax.rem(j, per_half) * tile, value)

        place(1, 4 * WIDTH - per_half * tile, gwout[...].astype(BF))


def run_layer(coords, lengths, normed, turned, grad_out, pieces):
    tokens = normed.shape[0]
    smem = pl.BlockSpec(memory_space=pltpu.SMEM)

    def whole(shape):
        return pl.BlockSpec(shape, lambda i: (0, 0))

    def by_seq(cols):
        return pl.BlockSpec((SEQ, cols), lambda i: (i, 0))

    return pl.pallas_call(
        layer_kernel,
        grid=(tokens // SEQ,),
        in_specs=[smem, smem, by_seq(WIDTH), by_seq(WIDTH)]
        + [whole(p.shape) for p in (turned, *pieces)],
        out_specs=[
            by_seq(4 * WIDTH),
            whole((WIDTH, 5 * WIDTH // 2)),
            whole((WIDTH, 5 * WIDTH // 2)),
            whole((4 * WIDTH, WIDTH)),
        ],
        out_shape=[
            jax.ShapeDtypeStruct((tokens, 4 * WIDTH), BF),
            jax.ShapeDtypeStruct((WIDTH, 5 * WIDTH // 2), BF),
            jax.ShapeDtypeStruct((WIDTH, 5 * WIDTH // 2), BF),
            jax.ShapeDtypeStruct((4 * WIDTH, WIDTH), BF),
        ],
        scratch_shapes=[
            pltpu.VMEM((WIDTH, 5 * WIDTH), BF),
            pltpu.VMEM((SEQ, WIDTH), F32),
            pltpu.VMEM((SEQ, 4 * WIDTH), F32),
            pltpu.VMEM((SEQ, 4 * WIDTH), BF),
            pltpu.VMEM((HEADS, SEQ, SEQ), BF),
            pltpu.VMEM((HEADS, SEQ, SEQ), BF),
            pltpu.VMEM((SEQ, WIDTH), F32),
            pltpu.VMEM((SEQ, WIDTH), BF),
            pltpu.VMEM((SEQ, WIDTH), BF),
            pltpu.VMEM((tokens, 4 * WIDTH), BF),
            pltpu.VMEM((WIDTH, WIDTH), F32),
        ],
        compiler_params=pltpu.CompilerParams(vmem_limit_bytes=56 * 1024 * 1024),
        cost_estimate=pl.CostEstimate(
            flops=20_000_000_000, bytes_accessed=20_000_000, transcendentals=8_000_000
        ),
        name="layer",
    )(coords, lengths, normed, grad_out, turned, *pieces)


def token_kernel(emb, go, gp, w, after, tokens, grads):
    chunk = 64
    grads[...] = dot_nn(gp[...], w[...])

    @pl.loop(0, SEQ // chunk)
    def _(i):
        rows = pl.ds(pl.multiple_of(i * chunk, chunk), chunk)
        xhat, rstd = normalise(emb[rows, :].astype(F32))
        back = norm_back(xhat, rstd, grads[rows, :])
        tokens[rows, :] = (back + go[rows, :].astype(F32)).astype(BF)


def run_tokens(embedded, grad_out, grad_proj, w, after):
    count = embedded.shape[0]

    def by_seq(cols):
        return pl.BlockSpec((SEQ, cols), lambda i: (i, 0))

    return pl.pallas_call(
        token_kernel,
        grid=(count // SEQ,),
        in_specs=[
            by_seq(WIDTH),
            by_seq(WIDTH),
            by_seq(4 * WIDTH),
            pl.BlockSpec((4 * WIDTH, WIDTH), lambda i: (0, 0)),
            pl.BlockSpec(memory_space=pl.ANY),
        ],
        out_specs=by_seq(WIDTH),
        out_shape=jax.ShapeDtypeStruct((count, WIDTH), BF),
        scratch_shapes=[pltpu.VMEM((SEQ, WIDTH), F32)],
        compiler_params=pltpu.CompilerParams(vmem_limit_bytes=56 * 1024 * 1024),
        cost_estimate=pl.CostEstimate(
            flops=4_300_000_000, bytes_accessed=16_000_000, transcendentals=2048
        ),
        name="token_grads",
    )(embedded, grad_out, grad_proj, w, after)


def bucket_kernel(bucket, labels, tokens, after, out):
    owners, total = out.shape[1], tokens.shape[0]
    tile = owners * CAP
    slot = lax.broadcasted_iota(jnp.int32, (tile, total), 0) + pl.program_id(0) * tile
    pick = jnp.where(slot == bucket[...], 1.0, 0.0).astype(BF)
    sums = dot_nn(pick, tokens[...]).astype(BF)
    marks = labels[...].astype(F32).astype(BF)
    for part in range(out.shape[0]):
        for owner in range(owners):
            cols = slice(part * 128, (part + 1) * 128)
            out[part, owner, 0:CAP, :] = sums[owner * CAP : (owner + 1) * CAP, cols]
            out[part, owner, CAP:PACKET, :] = jnp.broadcast_to(
                marks[owner : owner + 1, :], (PACKET - CAP, 128)
            )


def run_buckets(bucket, labels, tokens, parts, after):
    count, width = tokens.shape
    owners = labels.shape[0]
    per_step = 8
    return pl.pallas_call(
        bucket_kernel,
        grid=(owners // per_step,),
        in_specs=[
            pl.BlockSpec((1, count), lambda i: (0, 0)),
            pl.BlockSpec((per_step, 128), lambda i: (i, 0)),
            pl.BlockSpec((count, width), lambda i: (0, 0)),
            pl.BlockSpec(memory_space=pl.ANY),
        ],
        out_specs=pl.BlockSpec((parts, per_step, PACKET, 128), lambda i: (0, i, 0, 0)),
        out_shape=jax.ShapeDtypeStruct((parts, owners, PACKET, 128), BF),
        compiler_params=pltpu.CompilerParams(vmem_limit_bytes=56 * 1024 * 1024),
        cost_estimate=pl.CostEstimate(
            flops=4_300_000_000, bytes_accessed=6_000_000, transcendentals=0
        ),
        name="bucket_rows",
    )(bucket, labels, tokens, after)


def label_kernel(counts, offsets, rows, out):
    last = rows.shape[0] - 1

    @pl.loop(0, counts.shape[0])
    def _(owner):
        count, first = counts[owner], offsets[owner]
        for place in range(CAP):
            row = rows[jnp.minimum(first + place, last)]
            row = jnp.where(place < count, row, ROWS_DEV)
            out[owner, place] = lax.shift_right_logical(row, 6)
            out[owner, CAP + place] = jnp.bitwise_and(row, 63)


def run_labels(counts, offsets, rows):
    smem = pl.BlockSpec(memory_space=pltpu.SMEM)
    return pl.pallas_call(
        label_kernel,
        in_specs=[smem] * 3,
        out_specs=smem,
        out_shape=jax.ShapeDtypeStruct((counts.shape[0], 2 * CAP), jnp.int32),
        cost_estimate=pl.CostEstimate(flops=10_000, bytes_accessed=10_000, transcendentals=0),
        name="labels",
    )(counts, offsets, rows)


def scatter_kernel(rows, out, table, block, words, labels, sem):
    batch = 16
    marks = rows[:, CAP, :].astype(F32)
    marks = marks * 64.0 + pltpu.roll(marks, CAP, 1)
    words[...] = marks.astype(jnp.int32)
    copy = pltpu.make_async_copy(words, labels, sem)
    copy.start()

    @pl.loop(0, ROWS_DEV // 128)
    def _(i):
        table[pl.ds(pl.multiple_of(i * 128, 128), 128), :] = jnp.zeros((128, 128), F32)

    table[ROWS_DEV : ROWS_DEV + 8, :] = jnp.zeros((8, 128), F32)
    copy.wait()

    @pl.loop(0, rows.shape[0])
    def _(source):
        block[...] = rows[source, 0:CAP, :].astype(F32)

        def add_batch(start):
            places = range(start, start + batch)
            wheres = [labels[source, p] for p in places]
            sums = [
                table[pl.ds(w, 1), :] + block[p : p + 1, :] for p, w in zip(places, wheres)
            ]
            for w, s in zip(wheres, sums):
                table[pl.ds(w, 1), :] = s

        for start in range(0, CAP, batch):
            pl.when(labels[source, start] != ROWS_DEV)(functools.partial(add_batch, start))

    out[...] = table[0:ROWS_DEV, :]


def run_scatter(rows):
    sources, _, width = rows.shape
    whole = pl.BlockSpec(memory_space=pltpu.VMEM)
    return pl.pallas_call(
        scatter_kernel,
        in_specs=[whole],
        out_specs=whole,
        out_shape=jax.ShapeDtypeStruct((ROWS_DEV, width), F32),
        scratch_shapes=[
            pltpu.VMEM((ROWS_DEV + 8, width), F32),
            pltpu.VMEM((CAP, width), F32),
            pltpu.VMEM((sources, 2 * CAP), jnp.int32),
            pltpu.SMEM((sources, 2 * CAP), jnp.int32),
            pltpu.SemaphoreType.DMA,
        ],
        compiler_params=pltpu.CompilerParams(vmem_limit_bytes=32 * 1024 * 1024),
        cost_estimate=pl.CostEstimate(
            flops=2_000_000, bytes_accessed=6_000_000, transcendentals=0
        ),
        name="scatter",
    )(rows)


def ring(array, axis, size, shift):
    return lax.ppermute(array, axis, [(i, (i + shift) % size) for i in range(size)])


def swap_cores(array, count):
    return lax.ppermute(array, "table", [(i, i ^ 1) for i in range(count)])


def table_ring(array, stride, size, shift, count):
    pairs = []
    for i in range(count):
        place = (i // stride) % size
        pairs.append((i, i + (((place + shift) % size) - place) * stride))
    return lax.ppermute(array, "table", pairs)


def small_kernel(body, name, coords, arrays, outs, after=(), through=()):
    def kernel(place, *refs):
        first = len(arrays) + len(after) + len(through)
        body(place, *refs[: len(arrays)], *refs[first : first + len(outs)])

    whole = pl.BlockSpec(memory_space=pltpu.VMEM)
    return pl.pallas_call(
        kernel,
        in_specs=[pl.BlockSpec(memory_space=pltpu.SMEM)]
        + [whole] * len(arrays)
        + [pl.BlockSpec(memory_space=pl.ANY)] * (len(after) + len(through)),
        out_specs=[whole] * len(outs) + [pl.BlockSpec(memory_space=pl.ANY)] * len(through),
        out_shape=[jax.ShapeDtypeStruct(shape, kind) for shape, kind in outs]
        + [jax.ShapeDtypeStruct(a.shape, a.dtype) for a in through],
        input_output_aliases={
            1 + len(arrays) + len(after) + i: len(outs) + i for i in range(len(through))
        },
        compiler_params=pltpu.CompilerParams(vmem_limit_bytes=16 * 1024 * 1024),
        cost_estimate=pl.CostEstimate(
            flops=1_000_000, bytes_accessed=2_000_000, transcendentals=0
        ),
        name=name,
    )(coords, *arrays, *after, *through)


def block_rows(place, offset, rows):
    return pl.ds(pl.multiple_of(lax.rem(place + offset, 4) * rows, rows), rows)


def total(*terms):
    value = terms[0].astype(F32)
    for term in terms[1:]:
        value = value + term.astype(F32)
    return value.astype(BF)


def add_cores(coords, mine, theirs, far_a, far_b, right, left, own):
    me, rows = coords[0], own.shape[0]
    half = rows // 2
    far = block_rows(me, 2, rows)
    both = total(mine[far, :], theirs[far, :])
    far_a[...] = both[:half]
    far_b[...] = both[half:]
    for out, offset in ((right, 1), (left, 3), (own, 0)):
        part = block_rows(me, offset, rows)
        out[...] = total(mine[part, :], theirs[part, :])


def add_far(coords, right, left, from_left, from_right, to_right, to_left):
    half = from_left.shape[0]
    to_right[:half, :] = total(right[:half, :], from_left[...])
    to_right[half:, :] = right[half:, :]
    to_left[:half, :] = left[:half, :]
    to_left[half:, :] = total(left[half:, :], from_right[...])


def add_x(coords, own, from_left, from_right, scratch, right, left, far, mine):
    scratch[...] = total(own[...], from_left[...], from_right[...])
    for out, offset in ((right, 1), (left, 3), (far, 2), (mine, 0)):
        out[...] = scratch[block_rows(coords[2], offset, out.shape[0]), :]


def quarter(place, offset, rows, cols):
    index = lax.rem(place + offset, 4)
    return (
        pl.ds(pl.multiple_of(index // 2 * rows, rows), rows),
        pl.ds(pl.multiple_of(lax.rem(index, 2) * cols, cols), cols),
    )


def add_y(coords, own, from_left, from_right, from_far, scratch, right, left, far, mine):
    scratch[...] = total(own[...], from_left[...], from_right[...], from_far[...])
    for out, offset in ((right, 1), (left, 3), (far, 2), (mine, 0)):
        rows, cols = quarter(coords[3], offset, *out.shape)
        out[...] = scratch[rows, cols]


def add_z(coords, own, from_left, from_right, from_far, out):
    out[...] = total(own[...], from_left[...], from_right[...], from_far[...])


def join_z(coords, own, left, right, far, out):
    for piece, offset in ((own, 0), (left, 3), (right, 1), (far, 2)):
        rows, cols = quarter(coords[3], offset, *piece.shape)
        out[rows, cols] = piece[...]


def join_y(coords, own, left, right, far, out):
    for piece, offset in ((own, 0), (left, 3), (right, 1), (far, 2)):
        out[block_rows(coords[2], offset, piece.shape[0]), :] = piece[...]


def join_cores(factor, coords, own, theirs, share_in, share_out):
    core = coords[1]
    cut = own.shape[1]
    width = share_in.shape[1]

    def put(first, second):
        share_in[:, :cut] = first[...].astype(F32) * factor
        share_in[:, cut:] = second[:, : width - cut].astype(F32) * factor
        share_out[...] = second[:, width - cut :].astype(F32) * factor

    @pl.when(core == 0)
    def _():
        put(own, theirs)

    @pl.when(core == 1)
    def _():
        put(theirs, own)


def three_ways(shift, right, left, far):
    return shift(right, 1), shift(left, -1), shift(far, 2)


def per_device(
    embedded, grad_out, w_in, w_out, lengths, slot_of, local_rows, send_counts, send_offsets
):
    fsdp_count = lax.axis_size("fsdp")
    table_count = lax.axis_size("table")
    fsdp, table = lax.axis_index("fsdp"), lax.axis_index("table")
    core = lax.rem(table, 2)
    coords = jnp.stack([fsdp, core, table // 8, lax.rem(table // 2, 4)]).astype(jnp.int32)
    counts, offsets = send_counts[0], send_offsets[0]

    def along_x(array, shift):
        return ring(array, "fsdp", 4, shift)

    def along_y(array, shift):
        return table_ring(array, 8, 4, shift, table_count)

    def along_z(array, shift):
        return table_ring(array, 2, 4, shift, table_count)

    half = jnp.concatenate(
        [lax.dynamic_slice_in_dim(a, core * 64, 64, 0) for a in (w_in, w_out)], axis=1
    )
    low, high = along_x(half, 1), along_x(half, -1)
    labels = run_labels(counts, offsets, local_rows)
    low, high, labels = lax.optimization_barrier((low, high, labels))
    far_a, far_b = along_x(low[:32], 1), along_x(high[32:], -1)
    normed, turned = run_norm(embedded, labels)
    far_a, far_b, normed = lax.optimization_barrier((far_a, far_b, normed))
    low_o, high_o, far_ao, far_bo = (
        swap_cores(a, table_count) for a in (low, high, far_a, far_b)
    )
    pieces = [w_in, w_out, low, high, low_o, high_o, far_a, far_b, far_ao, far_bo]

    shift = jnp.where(
        slot_of[None, :] >= offsets[1:, None], CAP - counts[:-1, None], 0
    ).sum(axis=0)
    bucket = (slot_of + shift).reshape(1, -1)

    grad_proj, mine, other, w_full = run_layer(
        coords, lengths, normed, turned, grad_out, pieces
    )

    theirs = swap_cores(other, table_count)
    tokens = run_tokens(embedded, grad_out, grad_proj, w_full, other)

    rows, cols = mine.shape
    block, part = rows // 4, rows // 16
    far_a, far_b, right, left, own = small_kernel(
        add_cores,
        "add_cores",
        coords,
        (mine, theirs),
        [((block // 2, cols), BF)] * 2 + [((block, cols), BF)] * 3,
        after=(tokens,),
    )
    from_left, from_right = along_x(far_a, 1), along_x(far_b, -1)
    bucket_rows = run_buckets(bucket, labels, tokens, fsdp_count, own)
    to_right, to_left, bucket_rows = small_kernel(
        add_far,
        "add_far",
        coords,
        (right, left, from_left, from_right),
        [((block, cols), BF)] * 2,
        through=(bucket_rows,),
    )
    from_left, from_right = along_x(to_right, 1), along_x(to_left, -1)

    values = bucket_rows.reshape(fsdp_count * table_count, PACKET, 128)
    got = lax.all_to_all(values, BOTH, split_axis=0, concat_axis=0, tiled=True)

    _, right, left, far, own = small_kernel(
        add_x,
        "add_x",
        coords,
        (own, from_left, from_right),
        [((block, cols), BF)] + [((part, cols), BF)] * 4,
    )
    _, right, left, far, own = small_kernel(
        add_y,
        "add_y",
        coords,
        (own, *three_ways(along_y, right, left, far)),
        [((part, cols), BF)] + [((part // 2, cols // 2), BF)] * 4,
    )
    (own,) = small_kernel(
        add_z,
        "add_z",
        coords,
        (own, *three_ways(along_z, right, left, far)),
        [((part // 2, cols // 2), BF)],
    )
    (own,) = small_kernel(
        join_z,
        "join_z",
        coords,
        (own, *three_ways(along_z, own, own, own)),
        [((part, cols), BF)],
    )
    (own,) = small_kernel(
        join_y,
        "join_y",
        coords,
        (own, *three_ways(along_y, own, own, own)),
        [((block, cols), BF)],
    )
    factor = 1.0 / math.sqrt(embedded.shape[0] * fsdp_count * table_count)
    share_in, share_out = small_kernel(
        functools.partial(join_cores, factor),
        "join_cores",
        coords,
        (own, swap_cores(own, table_count)),
        [((block, 4 * WIDTH), F32), ((block, WIDTH), F32)],
    )

    grad_table = run_scatter(got)
    return (share_in, share_out, grad_table)


def solution(mesh):
    placed = (
        P(BOTH, None),
        P(BOTH, None),
        P("fsdp", None),
        P("fsdp", None),
        P(BOTH),
        P(BOTH),
        P(BOTH),
        P(BOTH, None),
        P(BOTH, None),
    )
    return jax.shard_map(
        per_device,
        mesh=mesh,
        in_specs=placed,
        out_specs=(P("fsdp", None), P("fsdp", None), P("table", "fsdp")),
        check_vma=False,
    )
```

```python
import functools
import math

import jax
import jax.numpy as jnp
from jax import lax
from jax.experimental import pallas as pl
from jax.experimental.pallas import tpu as pltpu
from jax.sharding import PartitionSpec as P

HEAD_DIM = 128
ROWS_DEV = 4096
CAP = 64
PACKET = 72
SEQ = 512
WIDTH = 512
HEADS = WIDTH // HEAD_DIM
HALF = SEQ // 2
EPS = 1e-05
BF = jnp.bfloat16
F32 = jnp.float32
BOTH = ("fsdp", "table")


def dot_nn(a, b):
    return lax.dot_general(a, b, (((1,), (0,)), ((), ())), preferred_element_type=F32)


def dot_nt(a, b):
    return lax.dot_general(a, b, (((1,), (1,)), ((), ())), preferred_element_type=F32)


def dot_tn(a, b):
    return lax.dot_general(a, b, (((0,), (0,)), ((), ())), preferred_element_type=F32)


def normalise(x):
    center = x - jnp.mean(x, axis=-1, keepdims=True)
    rstd = lax.rsqrt(jnp.mean(center * center, axis=-1, keepdims=True) + EPS)
    return center * rstd, rstd


def norm_back(xhat, rstd, cot):
    return rstd * (
        cot
        - jnp.mean(cot, axis=-1, keepdims=True)
        - xhat * jnp.mean(cot * xhat, axis=-1, keepdims=True)
    )


def norm_kernel(emb, after, normed, turned):
    xhat, _ = normalise(emb[...].astype(F32))
    normed[...] = xhat.astype(BF)
    turned[...] = normed[...].T


def run_norm(embedded, after):
    tokens = embedded.shape[0]
    return pl.pallas_call(
        norm_kernel,
        grid=(tokens // SEQ,),
        in_specs=[
            pl.BlockSpec((SEQ, WIDTH), lambda i: (i, 0)),
            pl.BlockSpec(memory_space=pl.ANY),
        ],
        out_specs=[
            pl.BlockSpec((SEQ, WIDTH), lambda i: (i, 0)),
            pl.BlockSpec((WIDTH, SEQ), lambda i: (0, i)),
        ],
        out_shape=[
            jax.ShapeDtypeStruct((tokens, WIDTH), BF),
            jax.ShapeDtypeStruct((WIDTH, tokens), BF),
        ],
        compiler_params=pltpu.CompilerParams(vmem_limit_bytes=56 * 1024 * 1024),
        cost_estimate=pl.CostEstimate(
            flops=20_000_000, bytes_accessed=6_000_000, transcendentals=2048
        ),
        name="norm",
    )(embedded, after)


def layer_kernel(
    coords, lens, normed, go, turned, own_in, own_out,
    low, high, low_o, high_o, far_a, far_b, far_ao, far_bo,
    gp, mine, other, w_turned,
    w, slope, hidden, probs, rates, mixed, cot, seq_sum, gp_all, gwout,
):
    step = pl.program_id(0)

    @pl.when(step == 0)
    def _():
        me, core = coords[0], coords[1]

        def put(shard, which, offset, piece):
            row = lax.rem(shard, 4) * 128 + which * 64 + offset
            w[pl.ds(pl.multiple_of(row, 32), piece.shape[0]), :] = piece[...]

        home = pl.ds(pl.multiple_of(me * 128, 128), 128)
        w[home, 0 : 4 * WIDTH] = own_in[...]
        w[home, 4 * WIDTH :] = own_out[...]
        put(me + 3, core, 0, low)
        put(me + 3, 1 - core, 0, low_o)
        put(me + 1, core, 0, high)
        put(me + 1, 1 - core, 0, high_o)
        put(me + 2, core, 0, far_a)
        put(me + 2, core, 32, far_b)
        put(me + 2, 1 - core, 0, far_ao)
        put(me + 2, 1 - core, 32, far_bo)
        gwout[...] = jnp.zeros_like(gwout)

        @pl.loop(0, 4)
        def _(i):
            cols = pl.ds(pl.multiple_of(i * WIDTH, WIDTH), WIDTH)
            w_turned[cols, :] = w[:, cols].T

    for block in range(4):
        cols = slice(block * WIDTH, (block + 1) * WIDTH)
        half = 0.5 * dot_nn(normed[...], w[:, cols])
        t = jnp.tanh(half)
        ht = half * t
        hidden[:, cols] = (half + ht).astype(BF)
        slope[:, cols] = 0.5 * ((1.0 + half) + t * (1.0 - ht))

    factor = 0.5 / math.sqrt(HEAD_DIM)

    def head_cols(block, head):
        return slice(block * WIDTH + head * HEAD_DIM, block * WIDTH + (head + 1) * HEAD_DIM)

    causal = lax.broadcasted_iota(jnp.int32, (HALF, HALF), 1) <= lax.broadcasted_iota(
        jnp.int32, (HALF, HALF), 0
    )
    for head in range(HEADS):
        v_cols, q_cols, k_cols = (head_cols(b, head) for b in (1, 2, 3))
        for qi in range(2):
            q_rows = slice(qi * HALF, (qi + 1) * HALF)
            for ki in range(qi + 1):
                k_rows = slice(ki * HALF, (ki + 1) * HALF)
                z = factor * dot_nt(hidden[q_rows, q_cols], hidden[k_rows, k_cols])
                t = jnp.tanh(z)
                zt = z * t
                prob = z + zt
                rate = (1.0 + z) + t * (1.0 - zt)
                if qi == ki:
                    prob = jnp.where(causal, prob, 0.0)
                    rate = jnp.where(causal, rate, 0.0)
                probs[head, q_rows, k_rows] = prob.astype(BF)
                rates[head, q_rows, k_rows] = rate.astype(BF)
            seen = slice(0, (qi + 1) * HALF)
            mixed[q_rows, head_cols(0, head)] = dot_nn(
                probs[head, q_rows, seen], hidden[seen, v_cols]
            )

    here = pl.ds(pl.multiple_of(step * SEQ, SEQ), SEQ)
    keep = lax.broadcasted_iota(jnp.int32, (SEQ, 1), 0) < lens[step]
    raw = jnp.where(keep, mixed[...] * (1.0 / SEQ), 0.0)
    xhat, rstd = normalise(raw)
    gate = hidden[:, 0:WIDTH].astype(F32)
    down = dot_nt(go[...], w[:, 4 * WIDTH :]).astype(BF).astype(F32)
    seq_sum[...] = (xhat * gate).astype(BF)
    grad_gate = ((down * xhat).astype(BF).astype(F32) * slope[:, 0:WIDTH]).astype(BF)
    gp[:, 0:WIDTH] = grad_gate
    gp_all[here, 0:WIDTH] = grad_gate
    back = norm_back(xhat, rstd, down * gate)
    cot[...] = jnp.where(keep, back * (1.0 / SEQ), 0.0).astype(BF)
    gwout[...] += dot_tn(seq_sum[...], go[...])

    def finish(value, rows, cols):
        grad = (value.astype(BF).astype(F32) * slope[rows, cols]).astype(BF)
        gp[rows, cols] = grad
        here = pl.ds(pl.multiple_of(step * SEQ + rows.start, HALF), rows.stop - rows.start)
        gp_all[here, cols] = grad

    top, low_half, whole = slice(0, HALF), slice(HALF, SEQ), slice(0, SEQ)
    for head in range(HEADS):
        v_cols, q_cols, k_cols = (head_cols(b, head) for b in (1, 2, 3))
        c_cols = head_cols(0, head)
        for q_rows, seen in ((top, top), (low_half, whole)):
            down = dot_nt(cot[q_rows, c_cols], hidden[seen, v_cols]).astype(BF)
            score = down * rates[head, q_rows, seen]
            rates[head, q_rows, seen] = score
            finish(factor * dot_nn(score, hidden[seen, k_cols]), q_rows, q_cols)
        for k_rows, seen in ((top, whole), (low_half, low_half)):
            finish(dot_tn(probs[head, seen, k_rows], cot[seen, c_cols]), k_rows, v_cols)
            finish(
                factor * dot_tn(rates[head, seen, k_rows], hidden[seen, q_cols]),
                k_rows,
                k_cols,
            )

    @pl.when(step == pl.num_programs(0) - 1)
    def _():
        tile, per_half = 256, 5
        core = coords[1]

        def place(half, col, value):
            cols = pl.ds(pl.multiple_of(col, tile), value.shape[1])

            @pl.when(half == core)
            def _():
                mine[:, cols] = value

            @pl.when(half != core)
            def _():
                other[:, cols] = value

        @pl.loop(0, 4 * WIDTH // tile)
        def _(j):
            cols = pl.ds(pl.multiple_of(j * tile, tile), tile)
            value = dot_nn(turned[...], gp_all[:, cols]).astype(BF)
            place(j // per_half, lax.rem(j, per_half) * tile, value)

        place(1, 4 * WIDTH - per_half * tile, gwout[...].astype(BF))


def run_layer(coords, lengths, normed, turned, grad_out, pieces):
    tokens = normed.shape[0]
    smem = pl.BlockSpec(memory_space=pltpu.SMEM)

    def whole(shape):
        return pl.BlockSpec(shape, lambda i: (0, 0))

    def by_seq(cols):
        return pl.BlockSpec((SEQ, cols), lambda i: (i, 0))

    return pl.pallas_call(
        layer_kernel,
        grid=(tokens // SEQ,),
        in_specs=[smem, smem, by_seq(WIDTH), by_seq(WIDTH)]
        + [whole(p.shape) for p in (turned, *pieces)],
        out_specs=[
            by_seq(4 * WIDTH),
            whole((WIDTH, 5 * WIDTH // 2)),
            whole((WIDTH, 5 * WIDTH // 2)),
            whole((4 * WIDTH, WIDTH)),
        ],
        out_shape=[
            jax.ShapeDtypeStruct((tokens, 4 * WIDTH), BF),
            jax.ShapeDtypeStruct((WIDTH, 5 * WIDTH // 2), BF),
            jax.ShapeDtypeStruct((WIDTH, 5 * WIDTH // 2), BF),
            jax.ShapeDtypeStruct((4 * WIDTH, WIDTH), BF),
        ],
        scratch_shapes=[
            pltpu.VMEM((WIDTH, 5 * WIDTH), BF),
            pltpu.VMEM((SEQ, 4 * WIDTH), F32),
            pltpu.VMEM((SEQ, 4 * WIDTH), BF),
            pltpu.VMEM((HEADS, SEQ, SEQ), BF),
            pltpu.VMEM((HEADS, SEQ, SEQ), BF),
            pltpu.VMEM((SEQ, WIDTH), F32),
            pltpu.VMEM((SEQ, WIDTH), BF),
            pltpu.VMEM((SEQ, WIDTH), BF),
            pltpu.VMEM((tokens, 4 * WIDTH), BF),
            pltpu.VMEM((WIDTH, WIDTH), F32),
        ],
        compiler_params=pltpu.CompilerParams(vmem_limit_bytes=56 * 1024 * 1024),
        cost_estimate=pl.CostEstimate(
            flops=20_000_000_000, bytes_accessed=20_000_000, transcendentals=8_000_000
        ),
        name="layer",
    )(coords, lengths, normed, grad_out, turned, *pieces)


def token_kernel(emb, go, gp, w, after, tokens, done):
    grads = dot_nn(gp[...], w[...])
    xhat, rstd = normalise(emb[...].astype(F32))
    back = norm_back(xhat, rstd, grads)
    tokens[...] = (back + go[...].astype(F32)).astype(BF)
    done[...] = jnp.zeros_like(done)


def run_tokens(embedded, grad_out, grad_proj, w, first, steps, after):
    def by_seq(cols):
        return pl.BlockSpec((SEQ, cols), lambda i: (i + first, 0))

    return pl.pallas_call(
        token_kernel,
        grid=(steps,),
        in_specs=[
            by_seq(WIDTH),
            by_seq(WIDTH),
            by_seq(4 * WIDTH),
            pl.BlockSpec((4 * WIDTH, WIDTH), lambda i: (0, 0)),
            pl.BlockSpec(memory_space=pl.ANY),
        ],
        out_specs=[
            pl.BlockSpec((SEQ, WIDTH), lambda i: (i, 0)),
            pl.BlockSpec((8, 128), lambda i: (0, 0)),
        ],
        out_shape=[
            jax.ShapeDtypeStruct((steps * SEQ, WIDTH), BF),
            jax.ShapeDtypeStruct((8, 128), F32),
        ],
        compiler_params=pltpu.CompilerParams(vmem_limit_bytes=56 * 1024 * 1024),
        cost_estimate=pl.CostEstimate(
            flops=1_000_000_000, bytes_accessed=4_000_000, transcendentals=2048
        ),
        name="token_grads",
    )(embedded, grad_out, grad_proj, w, after)


def bucket_kernel(bucket, labels, early, late, after, out):
    owners = out.shape[1]
    tile, count = owners * CAP, early.shape[0]
    slot = lax.broadcasted_iota(jnp.int32, (tile, count), 0) + pl.program_id(0) * tile

    def pick(start):
        return jnp.where(slot == bucket[:, start : start + count], 1.0, 0.0).astype(BF)

    sums = (dot_nn(pick(0), early[...]) + dot_nn(pick(count), late[...])).astype(BF)
    upper = lax.shift_right_logical(labels[...], 6)
    lower = jnp.bitwise_and(labels[...], 63)
    lane = lax.broadcasted_iota(jnp.int32, labels.shape, 1)
    marks = jnp.where(lane < CAP, upper, pltpu.roll(lower, CAP, 1)).astype(F32).astype(BF)
    for part in range(out.shape[0]):
        for owner in range(owners):
            cols = slice(part * 128, (part + 1) * 128)
            out[part, owner, 0:CAP, :] = sums[owner * CAP : (owner + 1) * CAP, cols]
            out[part, owner, CAP:PACKET, :] = jnp.broadcast_to(
                marks[owner : owner + 1, :], (PACKET - CAP, 128)
            )


def run_buckets(bucket, labels, early, late, parts, after):
    count, width = early.shape
    owners = labels.shape[0]
    per_step = 8
    whole = pl.BlockSpec((count, width), lambda i: (0, 0))
    return pl.pallas_call(
        bucket_kernel,
        grid=(owners // per_step,),
        in_specs=[
            pl.BlockSpec((1, 2 * count), lambda i: (0, 0)),
            pl.BlockSpec((per_step, 128), lambda i: (i, 0)),
            whole,
            whole,
            pl.BlockSpec(memory_space=pl.ANY),
        ],
        out_specs=pl.BlockSpec((parts, per_step, PACKET, 128), lambda i: (0, i, 0, 0)),
        out_shape=jax.ShapeDtypeStruct((parts, owners, PACKET, 128), BF),
        compiler_params=pltpu.CompilerParams(vmem_limit_bytes=56 * 1024 * 1024),
        cost_estimate=pl.CostEstimate(
            flops=200_000_000, bytes_accessed=1_000_000, transcendentals=0
        ),
        name="bucket_rows",
    )(bucket, labels, early, late, after)


def label_kernel(counts, offsets, rows, out):
    last = rows.shape[0] - 1

    @pl.loop(0, counts.shape[0])
    def _(owner):
        count, first = counts[owner], offsets[owner]
        for place in range(CAP):
            row = rows[jnp.minimum(first + place, last)]
            out[owner, place] = jnp.where(place < count, row, ROWS_DEV)


def run_labels(counts, offsets, rows):
    smem = pl.BlockSpec(memory_space=pltpu.SMEM)
    return pl.pallas_call(
        label_kernel,
        in_specs=[smem] * 3,
        out_specs=smem,
        out_shape=jax.ShapeDtypeStruct((counts.shape[0], 2 * CAP), jnp.int32),
        cost_estimate=pl.CostEstimate(flops=10_000, bytes_accessed=10_000, transcendentals=0),
        name="labels",
    )(counts, offsets, rows)


def scatter_kernel(first, last, rows, *refs):
    if first:
        even_in, odd_in, _, *refs = refs
    if last:
        out, token, even, odd, even_block, odd_block, words, labels, sem = refs
    else:
        even, odd, token, even_block, odd_block, words, labels, sem = refs
    batch = 16
    marks = rows[:, CAP, :].astype(F32)
    marks = marks * 64.0 + pltpu.roll(marks, CAP, 1)
    words[...] = marks.astype(jnp.int32)
    copy = pltpu.make_async_copy(words, labels, sem)
    copy.start()
    if first:
        even[...] = even_in[...]
        odd[...] = odd_in[...]
    else:
        even[...] = jnp.zeros_like(even)
        odd[...] = jnp.zeros_like(odd)
    copy.wait()

    @pl.loop(0, rows.shape[0] // 2)
    def _(pair):
        both = ((2 * pair, even, even_block), (2 * pair + 1, odd, odd_block))
        for source, _, block in both:
            block[...] = rows[source, 0:CAP, :].astype(F32)

        def add_batch(start):
            todo = []
            for source, table, block in both:
                for place in range(start, start + batch):
                    here = pl.ds(labels[source, place], 1)
                    todo.append((table, here, table[here, :] + block[place : place + 1, :]))
            for table, here, value in todo:
                table[here, :] = value

        for start in range(0, CAP, batch):
            used = jnp.minimum(labels[2 * pair, start], labels[2 * pair + 1, start])
            pl.when(used != ROWS_DEV)(functools.partial(add_batch, start))

    if last:
        out[...] = even[0:ROWS_DEV, :] + odd[0:ROWS_DEV, :]
    token[...] = jnp.zeros_like(token)


def run_scatter(rows, piece, pieces, tables=None, after=None):
    sources, packet, width = rows.shape
    count = sources // pieces
    first, last = piece > 0, piece == pieces - 1
    whole = pl.BlockSpec(memory_space=pltpu.VMEM)
    table = jax.ShapeDtypeStruct((ROWS_DEV + 8, width), F32)
    scratch = [
        pltpu.VMEM((CAP, width), F32),
        pltpu.VMEM((CAP, width), F32),
        pltpu.VMEM((count, 2 * CAP), jnp.int32),
        pltpu.SMEM((count, 2 * CAP), jnp.int32),
        pltpu.SemaphoreType.DMA,
    ]
    if last:
        out_shape = [jax.ShapeDtypeStruct((ROWS_DEV, width), F32)]
        scratch = [pltpu.VMEM(table.shape, F32), pltpu.VMEM(table.shape, F32)] + scratch
    else:
        out_shape = [table, table]
    out_shape.append(jax.ShapeDtypeStruct((8, 128), F32))
    return pl.pallas_call(
        functools.partial(scatter_kernel, first, last),
        grid=(1,),
        in_specs=[pl.BlockSpec((count, packet, width), lambda i: (piece, 0, 0))]
        + ([whole, whole, pl.BlockSpec(memory_space=pl.ANY)] if first else []),
        out_specs=[whole] * len(out_shape),
        out_shape=out_shape,
        scratch_shapes=scratch,
        compiler_params=pltpu.CompilerParams(vmem_limit_bytes=24 * 1024 * 1024),
        cost_estimate=pl.CostEstimate(
            flops=2_000_000, bytes_accessed=6_000_000, transcendentals=0
        ),
        name="scatter",
    )(rows, *((*tables, after) if first else ()))


def ring(array, axis, size, shift):
    return lax.ppermute(array, axis, [(i, (i + shift) % size) for i in range(size)])


def table_ring(array, stride, size, shift, count):
    pairs = []
    for i in range(count):
        place = (i // stride) % size
        pairs.append((i, i + (((place + shift) % size) - place) * stride))
    return lax.ppermute(array, "table", pairs)


def swap(array, bit, count):
    return lax.ppermute(array, "table", [(i, i ^ bit) for i in range(count)])


def small_kernel(body, name, coords, arrays, outs, after=(), through=(), limit=16):
    def kernel(place, *refs):
        first = len(arrays) + len(after) + len(through)
        body(place, *refs[: len(arrays)], *refs[first : first + len(outs)])

    whole = pl.BlockSpec(memory_space=pltpu.VMEM)
    return pl.pallas_call(
        kernel,
        in_specs=[pl.BlockSpec(memory_space=pltpu.SMEM)]
        + [whole] * len(arrays)
        + [pl.BlockSpec(memory_space=pl.ANY)] * (len(after) + len(through)),
        out_specs=[whole] * len(outs) + [pl.BlockSpec(memory_space=pl.ANY)] * len(through),
        out_shape=[jax.ShapeDtypeStruct(shape, kind) for shape, kind in outs]
        + [jax.ShapeDtypeStruct(a.shape, a.dtype) for a in through],
        input_output_aliases={
            1 + len(arrays) + len(after) + i: len(outs) + i for i in range(len(through))
        },
        compiler_params=pltpu.CompilerParams(vmem_limit_bytes=limit * 1024 * 1024),
        cost_estimate=pl.CostEstimate(
            flops=1_000_000, bytes_accessed=2_000_000, transcendentals=0
        ),
        name=name,
    )(coords, *arrays, *after, *through)


def block_rows(place, offset, rows):
    return pl.ds(pl.multiple_of(lax.rem(place + offset, 4) * rows, rows), rows)


def total(*terms):
    value = terms[0].astype(F32)
    for term in terms[1:]:
        value = value + term.astype(F32)
    return value.astype(BF)


def add_cores(coords, mine, theirs, right, left, far, own, done):
    done[...] = jnp.zeros_like(done)
    rows = own.shape[0]
    for out, offset in ((right, 1), (left, 3), (far, 2), (own, 0)):
        part = block_rows(coords[0], offset, rows)
        out[...] = total(mine[part, :], theirs[part, :])


def add_x(coords, own, from_left, from_right, from_far, scratch, right, left, far, mine):
    scratch[...] = total(own[...], from_left[...], from_right[...], from_far[...])
    for out, offset in ((right, 1), (left, 3), (far, 2), (mine, 0)):
        out[...] = scratch[block_rows(coords[2], offset, out.shape[0]), :]


def add_all(coords, *refs):
    refs[-1][...] = total(*(ref[...] for ref in refs[:-1]))


def join_y(coords, own, left, right, far, out):
    for piece, offset in ((own, 0), (left, 3), (right, 1), (far, 2)):
        out[block_rows(coords[2], offset, piece.shape[0]), :] = piece[...]


def join_cores(factor, coords, own, theirs, share_in, share_out):
    core = coords[1]
    cut = own.shape[1]
    width = share_in.shape[1]

    def put(first, second):
        share_in[:, :cut] = first[...].astype(F32) * factor
        share_in[:, cut:] = second[:, : width - cut].astype(F32) * factor
        share_out[...] = second[:, width - cut :].astype(F32) * factor

    @pl.when(core == 0)
    def _():
        put(own, theirs)

    @pl.when(core == 1)
    def _():
        put(theirs, own)


def per_device(
    embedded, grad_out, w_in, w_out, lengths, slot_of, local_rows, send_counts, send_offsets
):
    fsdp_count = lax.axis_size("fsdp")
    table_count = lax.axis_size("table")
    fsdp, table = lax.axis_index("fsdp"), lax.axis_index("table")
    core = lax.rem(table, 2)
    coords = jnp.stack([fsdp, core, table // 8, lax.rem(table // 2, 4)]).astype(jnp.int32)
    counts, offsets = send_counts[0], send_offsets[0]

    def along_x(array, shift):
        return ring(array, "fsdp", 4, shift)

    def along_y(array, shift):
        return table_ring(array, 8, 4, shift, table_count)

    def three_ways(along, right, left, far):
        return along(right, 1), along(left, -1), along(far, 2)

    half = jnp.concatenate(
        [lax.dynamic_slice_in_dim(a, core * 64, 64, 0) for a in (w_in, w_out)], axis=1
    )
    low, high = along_x(half, 1), along_x(half, -1)
    labels = run_labels(counts, offsets, local_rows)
    low, high, labels = lax.optimization_barrier((low, high, labels))
    far_a, far_b = along_x(low[:32], 1), along_x(high[32:], -1)
    normed, turned = run_norm(embedded, labels)
    far_a, far_b, normed = lax.optimization_barrier((far_a, far_b, normed))
    low_o, high_o, far_ao, far_bo = (
        swap(a, 1, table_count) for a in (low, high, far_a, far_b)
    )
    pieces = [w_in, w_out, low, high, low_o, high_o, far_a, far_b, far_ao, far_bo]

    shift = jnp.where(
        slot_of[None, :] >= offsets[1:, None], CAP - counts[:-1, None], 0
    ).sum(axis=0)
    bucket = (slot_of + shift).reshape(1, -1)

    grad_proj, mine, other, w_full = run_layer(
        coords, lengths, normed, turned, grad_out, pieces
    )

    theirs = swap(other, 1, table_count)
    half = embedded.shape[0] // SEQ // 2
    early, done = run_tokens(embedded, grad_out, grad_proj, w_full, 0, half, other)

    rows, cols = mine.shape
    block = rows // 4
    mark = ((8, 128), F32)
    right, left, far, own, done = small_kernel(
        add_cores,
        "add_cores",
        coords,
        (mine, theirs),
        [((block, cols), BF)] * 4 + [mark],
        after=(done,),
    )
    from_x = three_ways(along_x, right, left, far)
    late, done = run_tokens(embedded, grad_out, grad_proj, w_full, half, half, done)
    bucket_rows = run_buckets(bucket, labels, early, late, fsdp_count, done)
    part = block // 4
    _, right, left, far, own, bucket_rows = small_kernel(
        add_x,
        "add_x",
        coords,
        (own, *from_x),
        [((block, cols), BF)] + [((part, cols), BF)] * 4,
        through=(bucket_rows,),
        limit=58,
    )
    from_y = three_ways(along_y, right, left, far)
    one = [((part, cols), BF)]
    values = bucket_rows.reshape(fsdp_count * table_count, PACKET, 128)
    got = lax.all_to_all(values, BOTH, split_axis=0, concat_axis=0, tiled=True)

    (own,) = small_kernel(add_all, "add_y", coords, (own, *from_y), one)
    from_z = swap(own, 2, table_count)
    *tables, token = run_scatter(got, 0, 4)
    (own,) = small_kernel(add_all, "add_z_low", coords, (own, from_z), one, after=(token,))
    from_z = swap(own, 4, table_count)
    *tables, token = run_scatter(got, 1, 4, tables, own)
    (own,) = small_kernel(add_all, "add_z_high", coords, (own, from_z), one, after=(token,))
    from_y = three_ways(along_y, own, own, own)
    *tables, token = run_scatter(got, 2, 4, tables, own)
    (own,) = small_kernel(
        join_y, "join_y", coords, (own, *from_y), [((block, cols), BF)], after=(token,)
    )
    theirs = swap(own, 1, table_count)
    (grad_table, token) = run_scatter(got, 3, 4, tables, own)
    factor = 1.0 / math.sqrt(embedded.shape[0] * fsdp_count * table_count)
    share_in, share_out = small_kernel(
        functools.partial(join_cores, factor),
        "join_cores",
        coords,
        (own, theirs),
        [((block, 4 * WIDTH), F32), ((block, WIDTH), F32)],
        after=(token,),
    )
    return (share_in, share_out, grad_table)


def solution(mesh):
    placed = (
        P(BOTH, None),
        P(BOTH, None),
        P("fsdp", None),
        P("fsdp", None),
        P(BOTH),
        P(BOTH),
        P(BOTH),
        P(BOTH, None),
        P(BOTH, None),
    )
    return jax.shard_map(
        per_device,
        mesh=mesh,
        in_specs=placed,
        out_specs=(P("fsdp", None), P("fsdp", None), P("table", "fsdp")),
        check_vma=False,
    )
```

```python
import functools
import math

import jax
import jax.numpy as jnp
from jax import lax
from jax.experimental import pallas as pl
from jax.experimental.pallas import tpu as pltpu
from jax.sharding import PartitionSpec as P

HEAD_DIM = 128
ROWS_DEV = 4096
CAP = 64
PACKET = 72
SEQ = 512
WIDTH = 512
HEADS = WIDTH // HEAD_DIM
HALF = SEQ // 2
EPS = 1e-05
BF = jnp.bfloat16
F32 = jnp.float32
BOTH = ("fsdp", "table")


def dot_nn(a, b):
    return lax.dot_general(a, b, (((1,), (0,)), ((), ())), preferred_element_type=F32)


def dot_nt(a, b):
    return lax.dot_general(a, b, (((1,), (1,)), ((), ())), preferred_element_type=F32)


def dot_tn(a, b):
    return lax.dot_general(a, b, (((0,), (0,)), ((), ())), preferred_element_type=F32)


def normalise(x):
    center = x - jnp.mean(x, axis=-1, keepdims=True)
    rstd = lax.rsqrt(jnp.mean(center * center, axis=-1, keepdims=True) + EPS)
    return center * rstd, rstd


def norm_back(xhat, rstd, cot):
    return rstd * (
        cot
        - jnp.mean(cot, axis=-1, keepdims=True)
        - xhat * jnp.mean(cot * xhat, axis=-1, keepdims=True)
    )


def norm_kernel(emb, *refs):
    normed, turned = refs[-2:]
    xhat, _ = normalise(emb[...].astype(F32))
    normed[...] = xhat.astype(BF)
    turned[...] = normed[...].T


def run_norm(embedded, after, half, given=()):
    tokens = embedded.shape[0]
    steps = tokens // SEQ // 2
    first = half * steps
    anywhere = pl.BlockSpec(memory_space=pl.ANY)
    return pl.pallas_call(
        norm_kernel,
        grid=(steps,),
        in_specs=[pl.BlockSpec((SEQ, WIDTH), lambda i: (i + first, 0)), anywhere]
        + [anywhere] * len(given),
        out_specs=[
            pl.BlockSpec((SEQ, WIDTH), lambda i: (i + first, 0)),
            pl.BlockSpec((WIDTH, SEQ), lambda i: (0, i + first)),
        ],
        out_shape=[
            jax.ShapeDtypeStruct((tokens, WIDTH), BF),
            jax.ShapeDtypeStruct((WIDTH, tokens), BF),
        ],
        input_output_aliases={2 + i: i for i in range(len(given))},
        compiler_params=pltpu.CompilerParams(vmem_limit_bytes=56 * 1024 * 1024),
        cost_estimate=pl.CostEstimate(
            flops=10_000_000, bytes_accessed=3_000_000, transcendentals=1024
        ),
        name="norm",
    )(embedded, after, *given)


def layer_kernel(
    coords, lens, normed, go, emb, own_in, own_out,
    low, high, low_o, high_o, far_a, far_b, far_ao, far_bo,
    gp, tokens, gwout,
    w, w_turned, slope, hidden, probs, rates, mixed, cot, seq_sum,
):
    step = pl.program_id(0)

    @pl.when(step == 0)
    def _():
        me, core = coords[0], coords[1]

        def put(shard, which, offset, piece):
            row = lax.rem(shard, 4) * 128 + which * 64 + offset
            w[pl.ds(pl.multiple_of(row, 32), piece.shape[0]), :] = piece[...]

        home = pl.ds(pl.multiple_of(me * 128, 128), 128)
        w[home, 0 : 4 * WIDTH] = own_in[...]
        w[home, 4 * WIDTH :] = own_out[...]
        put(me + 3, core, 0, low)
        put(me + 3, 1 - core, 0, low_o)
        put(me + 1, core, 0, high)
        put(me + 1, 1 - core, 0, high_o)
        put(me + 2, core, 0, far_a)
        put(me + 2, core, 32, far_b)
        put(me + 2, 1 - core, 0, far_ao)
        put(me + 2, 1 - core, 32, far_bo)
        gwout[...] = jnp.zeros_like(gwout)

        @pl.loop(0, 4)
        def _(i):
            cols = pl.ds(pl.multiple_of(i * WIDTH, WIDTH), WIDTH)
            w_turned[cols, :] = w[:, cols].T

    for block in range(4):
        cols = slice(block * WIDTH, (block + 1) * WIDTH)
        half = 0.5 * dot_nn(normed[...], w[:, cols])
        t = jnp.tanh(half)
        ht = half * t
        hidden[:, cols] = (half + ht).astype(BF)
        slope[:, cols] = 0.5 * ((1.0 + half) + t * (1.0 - ht))

    factor = 0.5 / math.sqrt(HEAD_DIM)

    def head_cols(block, head):
        return slice(block * WIDTH + head * HEAD_DIM, block * WIDTH + (head + 1) * HEAD_DIM)

    causal = lax.broadcasted_iota(jnp.int32, (HALF, HALF), 1) <= lax.broadcasted_iota(
        jnp.int32, (HALF, HALF), 0
    )
    for head in range(HEADS):
        v_cols, q_cols, k_cols = (head_cols(b, head) for b in (1, 2, 3))
        for qi in range(2):
            q_rows = slice(qi * HALF, (qi + 1) * HALF)
            for ki in range(qi + 1):
                k_rows = slice(ki * HALF, (ki + 1) * HALF)
                z = factor * dot_nt(hidden[q_rows, q_cols], hidden[k_rows, k_cols])
                t = jnp.tanh(z)
                zt = z * t
                prob = z + zt
                rate = (1.0 + z) + t * (1.0 - zt)
                if qi == ki:
                    prob = jnp.where(causal, prob, 0.0)
                    rate = jnp.where(causal, rate, 0.0)
                probs[head, q_rows, k_rows] = prob.astype(BF)
                rates[head, q_rows, k_rows] = rate.astype(BF)
            seen = slice(0, (qi + 1) * HALF)
            mixed[q_rows, head_cols(0, head)] = dot_nn(
                probs[head, q_rows, seen], hidden[seen, v_cols]
            )

    keep = lax.broadcasted_iota(jnp.int32, (SEQ, 1), 0) < lens[step]
    raw = jnp.where(keep, mixed[...] * (1.0 / SEQ), 0.0)
    xhat, rstd = normalise(raw)
    gate = hidden[:, 0:WIDTH].astype(F32)
    down = dot_nt(go[...], w[:, 4 * WIDTH :]).astype(BF).astype(F32)
    seq_sum[...] = (xhat * gate).astype(BF)
    grad_gate = ((down * xhat).astype(BF).astype(F32) * slope[:, 0:WIDTH]).astype(BF)
    gp[:, 0:WIDTH] = grad_gate
    back = norm_back(xhat, rstd, down * gate)
    cot[...] = jnp.where(keep, back * (1.0 / SEQ), 0.0).astype(BF)
    gwout[...] += dot_tn(seq_sum[...], go[...])

    def finish(value, rows, cols):
        grad = (value.astype(BF).astype(F32) * slope[rows, cols]).astype(BF)
        gp[rows, cols] = grad

    top, low_half, whole = slice(0, HALF), slice(HALF, SEQ), slice(0, SEQ)
    for head in range(HEADS):
        v_cols, q_cols, k_cols = (head_cols(b, head) for b in (1, 2, 3))
        c_cols = head_cols(0, head)
        for q_rows, seen in ((top, top), (low_half, whole)):
            down = dot_nt(cot[q_rows, c_cols], hidden[seen, v_cols]).astype(BF)
            score = down * rates[head, q_rows, seen]
            rates[head, q_rows, seen] = score
            finish(factor * dot_nn(score, hidden[seen, k_cols]), q_rows, q_cols)
        for k_rows, seen in ((top, whole), (low_half, low_half)):
            finish(dot_tn(probs[head, seen, k_rows], cot[seen, c_cols]), k_rows, v_cols)
            finish(
                factor * dot_tn(rates[head, seen, k_rows], hidden[seen, q_cols]),
                k_rows,
                k_cols,
            )

    xhat, rstd = normalise(emb[...].astype(F32))
    back = norm_back(xhat, rstd, dot_nn(gp[...], w_turned[...]))
    tokens[...] = (back + go[...].astype(F32)).astype(BF)


def run_layer(coords, lengths, normed, embedded, grad_out, pieces):
    tokens = normed.shape[0]
    smem = pl.BlockSpec(memory_space=pltpu.SMEM)

    def whole(shape):
        return pl.BlockSpec(shape, lambda i: (0, 0))

    def by_seq(cols):
        return pl.BlockSpec((SEQ, cols), lambda i: (i, 0))

    return pl.pallas_call(
        layer_kernel,
        grid=(tokens // SEQ,),
        in_specs=[smem, smem] + [by_seq(WIDTH)] * 3 + [whole(p.shape) for p in pieces],
        out_specs=[by_seq(4 * WIDTH), by_seq(WIDTH), whole((WIDTH, WIDTH))],
        out_shape=[
            jax.ShapeDtypeStruct((tokens, 4 * WIDTH), BF),
            jax.ShapeDtypeStruct((tokens, WIDTH), BF),
            jax.ShapeDtypeStruct((WIDTH, WIDTH), F32),
        ],
        scratch_shapes=[
            pltpu.VMEM((WIDTH, 5 * WIDTH), BF),
            pltpu.VMEM((4 * WIDTH, WIDTH), BF),
            pltpu.VMEM((SEQ, 4 * WIDTH), F32),
            pltpu.VMEM((SEQ, 4 * WIDTH), BF),
            pltpu.VMEM((HEADS, SEQ, SEQ), BF),
            pltpu.VMEM((HEADS, SEQ, SEQ), BF),
            pltpu.VMEM((SEQ, WIDTH), F32),
            pltpu.VMEM((SEQ, WIDTH), BF),
            pltpu.VMEM((SEQ, WIDTH), BF),
        ],
        compiler_params=pltpu.CompilerParams(vmem_limit_bytes=56 * 1024 * 1024),
        cost_estimate=pl.CostEstimate(
            flops=20_000_000_000, bytes_accessed=20_000_000, transcendentals=8_000_000
        ),
        name="layer",
    )(coords, lengths, normed, grad_out, embedded, *pieces)


def weight_kernel(coords, turned, gp, gwout, after, mine, other):
    step = pl.program_id(0)
    core, half = coords[1], step // 2
    cols = pl.ds(pl.multiple_of(lax.rem(step, 2) * WIDTH, WIDTH), WIDTH)
    value = dot_nn(turned[...], gp[...]).astype(BF)

    @pl.when(half == core)
    def _():
        mine[:, cols] = value

    @pl.when(half != core)
    def _():
        other[:, cols] = value

    @pl.when(step == 0)
    def _():
        sides = gwout[...].astype(BF)
        first, second = sides[:, : WIDTH // 2], sides[:, WIDTH // 2 :]
        mine[:, 2 * WIDTH :] = jnp.where(core == 0, first, second)
        other[:, 2 * WIDTH :] = jnp.where(core == 0, second, first)


def run_weights(coords, turned, grad_proj, gwout, after):
    tokens = turned.shape[1]
    half = pl.BlockSpec((WIDTH, 5 * WIDTH // 2), lambda i: (0, 0))
    return pl.pallas_call(
        weight_kernel,
        grid=(4,),
        in_specs=[
            pl.BlockSpec(memory_space=pltpu.SMEM),
            pl.BlockSpec((WIDTH, tokens), lambda i: (0, 0)),
            pl.BlockSpec((tokens, WIDTH), lambda i: (0, i)),
            pl.BlockSpec((WIDTH, WIDTH), lambda i: (0, 0)),
            pl.BlockSpec(memory_space=pl.ANY),
        ],
        out_specs=[half, half],
        out_shape=[jax.ShapeDtypeStruct((WIDTH, 5 * WIDTH // 2), BF)] * 2,
        compiler_params=pltpu.CompilerParams(vmem_limit_bytes=56 * 1024 * 1024),
        cost_estimate=pl.CostEstimate(
            flops=4_300_000_000, bytes_accessed=13_000_000, transcendentals=0
        ),
        name="weight_grads",
    )(coords, turned, grad_proj, gwout, after)


def bucket_kernel(bucket, labels, tokens, out):
    owners = out.shape[1]
    tile, count = owners * CAP, tokens.shape[0]
    slot = lax.broadcasted_iota(jnp.int32, (tile, count), 0) + pl.program_id(0) * tile
    pick = jnp.where(slot == bucket[...], 1.0, 0.0).astype(BF)
    sums = dot_nn(pick, tokens[...]).astype(BF)
    upper = lax.shift_right_logical(labels[...], 6)
    lower = jnp.bitwise_and(labels[...], 63)
    lane = lax.broadcasted_iota(jnp.int32, labels.shape, 1)
    marks = jnp.where(lane < CAP, upper, pltpu.roll(lower, CAP, 1)).astype(F32).astype(BF)
    for part in range(out.shape[0]):
        for owner in range(owners):
            cols = slice(part * 128, (part + 1) * 128)
            out[part, owner, 0:CAP, :] = sums[owner * CAP : (owner + 1) * CAP, cols]
            out[part, owner, CAP:PACKET, :] = jnp.broadcast_to(
                marks[owner : owner + 1, :], (PACKET - CAP, 128)
            )


def run_buckets(bucket, labels, tokens, parts):
    count, width = tokens.shape
    owners = labels.shape[0]
    per_step = 8
    return pl.pallas_call(
        bucket_kernel,
        grid=(owners // per_step,),
        in_specs=[
            pl.BlockSpec((1, count), lambda i: (0, 0)),
            pl.BlockSpec((per_step, 128), lambda i: (i, 0)),
            pl.BlockSpec((count, width), lambda i: (0, 0)),
        ],
        out_specs=pl.BlockSpec((parts, per_step, PACKET, 128), lambda i: (0, i, 0, 0)),
        out_shape=jax.ShapeDtypeStruct((parts, owners, PACKET, 128), BF),
        compiler_params=pltpu.CompilerParams(vmem_limit_bytes=56 * 1024 * 1024),
        cost_estimate=pl.CostEstimate(
            flops=200_000_000, bytes_accessed=1_000_000, transcendentals=0
        ),
        name="bucket_rows",
    )(bucket, labels, tokens)


def label_kernel(counts, offsets, rows, out):
    lane = lax.broadcasted_iota(jnp.int32, (8, 128), 1)
    for owner in range(out.shape[0]):
        count, first = counts[owner], offsets[owner]
        start = lax.rem(first, 128)
        near = pltpu.roll(rows[pl.ds(first // 128, 8), :], lax.rem(128 - start, 128), 1)
        taken = jnp.where(lane[0:1] < 128 - start, near[0:1], near[1:2])
        out[owner : owner + 1, :] = jnp.where(lane[0:1] < count, taken, ROWS_DEV)


def run_labels(counts, offsets, rows):
    smem = pl.BlockSpec(memory_space=pltpu.SMEM)
    whole = pl.BlockSpec(memory_space=pltpu.VMEM)
    lines = -(-rows.shape[0] // 128) + 8
    rows = jnp.pad(rows, (0, lines * 128 - rows.shape[0])).reshape(lines, 128)
    return pl.pallas_call(
        label_kernel,
        in_specs=[smem, smem, whole],
        out_specs=whole,
        out_shape=jax.ShapeDtypeStruct((counts.shape[0], 2 * CAP), jnp.int32),
        cost_estimate=pl.CostEstimate(flops=10_000, bytes_accessed=10_000, transcendentals=0),
        name="labels",
    )(counts, offsets, rows)


def scatter_kernel(first, last, rows, *refs):
    if first:
        even_in, odd_in, _, *refs = refs
    if last:
        out, token, even, odd, even_block, odd_block, words, labels, sem = refs
    else:
        even, odd, token, even_block, odd_block, words, labels, sem = refs
    batch = 16
    marks = rows[:, CAP, :].astype(F32)
    marks = marks * 64.0 + pltpu.roll(marks, CAP, 1)
    words[...] = marks.astype(jnp.int32)
    copy = pltpu.make_async_copy(words, labels, sem)
    copy.start()
    if first:
        even[...] = even_in[...]
        odd[...] = odd_in[...]
    else:
        even[...] = jnp.zeros_like(even)
        odd[...] = jnp.zeros_like(odd)
    copy.wait()

    @pl.loop(0, rows.shape[0] // 2)
    def _(pair):
        both = ((2 * pair, even, even_block), (2 * pair + 1, odd, odd_block))
        for source, _, block in both:
            block[...] = rows[source, 0:CAP, :].astype(F32)

        def add_batch(start):
            todo = []
            for source, table, block in both:
                for place in range(start, start + batch):
                    here = pl.ds(labels[source, place], 1)
                    todo.append((table, here, table[here, :] + block[place : place + 1, :]))
            for table, here, value in todo:
                table[here, :] = value

        for start in range(0, CAP, batch):
            used = jnp.minimum(labels[2 * pair, start], labels[2 * pair + 1, start])
            pl.when(used != ROWS_DEV)(functools.partial(add_batch, start))

    if last:
        out[...] = even[0:ROWS_DEV, :] + odd[0:ROWS_DEV, :]
    token[...] = jnp.zeros_like(token)


def run_scatter(rows, start, count, tables=None, after=None):
    sources, packet, width = rows.shape
    first, last = start > 0, start + count == sources
    whole = pl.BlockSpec(memory_space=pltpu.VMEM)
    table = jax.ShapeDtypeStruct((ROWS_DEV + 8, width), F32)
    scratch = [
        pltpu.VMEM((CAP, width), F32),
        pltpu.VMEM((CAP, width), F32),
        pltpu.VMEM((count, 2 * CAP), jnp.int32),
        pltpu.SMEM((count, 2 * CAP), jnp.int32),
        pltpu.SemaphoreType.DMA,
    ]
    if last:
        out_shape = [jax.ShapeDtypeStruct((ROWS_DEV, width), F32)]
        scratch = [pltpu.VMEM(table.shape, F32), pltpu.VMEM(table.shape, F32)] + scratch
    else:
        out_shape = [table, table]
    out_shape.append(jax.ShapeDtypeStruct((8, 128), F32))
    return pl.pallas_call(
        functools.partial(scatter_kernel, first, last),
        grid=(1,),
        in_specs=[pl.BlockSpec((count, packet, width), lambda i: (start // count, 0, 0))]
        + ([whole, whole, pl.BlockSpec(memory_space=pl.ANY)] if first else []),
        out_specs=[whole] * len(out_shape),
        out_shape=out_shape,
        scratch_shapes=scratch,
        compiler_params=pltpu.CompilerParams(vmem_limit_bytes=24 * 1024 * 1024),
        cost_estimate=pl.CostEstimate(
            flops=2_000_000, bytes_accessed=6_000_000, transcendentals=0
        ),
        name="scatter",
    )(rows, *((*tables, after) if first else ()))


def ring(array, axis, size, shift):
    return lax.ppermute(array, axis, [(i, (i + shift) % size) for i in range(size)])


def table_ring(array, stride, size, shift, count):
    pairs = []
    for i in range(count):
        place = (i // stride) % size
        pairs.append((i, i + (((place + shift) % size) - place) * stride))
    return lax.ppermute(array, "table", pairs)


def swap(array, bit, count):
    return lax.ppermute(array, "table", [(i, i ^ bit) for i in range(count)])


def small_kernel(body, name, coords, arrays, outs, after=(), through=(), limit=16):
    def kernel(place, *refs):
        first = len(arrays) + len(after) + len(through)
        body(place, *refs[: len(arrays)], *refs[first : first + len(outs)])

    whole = pl.BlockSpec(memory_space=pltpu.VMEM)
    return pl.pallas_call(
        kernel,
        in_specs=[pl.BlockSpec(memory_space=pltpu.SMEM)]
        + [whole] * len(arrays)
        + [pl.BlockSpec(memory_space=pl.ANY)] * (len(after) + len(through)),
        out_specs=[whole] * len(outs) + [pl.BlockSpec(memory_space=pl.ANY)] * len(through),
        out_shape=[jax.ShapeDtypeStruct(shape, kind) for shape, kind in outs]
        + [jax.ShapeDtypeStruct(a.shape, a.dtype) for a in through],
        input_output_aliases={
            1 + len(arrays) + len(after) + i: len(outs) + i for i in range(len(through))
        },
        compiler_params=pltpu.CompilerParams(vmem_limit_bytes=limit * 1024 * 1024),
        cost_estimate=pl.CostEstimate(
            flops=1_000_000, bytes_accessed=2_000_000, transcendentals=0
        ),
        name=name,
    )(coords, *arrays, *after, *through)


def block_rows(place, offset, rows):
    return pl.ds(pl.multiple_of(lax.rem(place + offset, 4) * rows, rows), rows)


def total(*terms):
    value = terms[0].astype(F32)
    for term in terms[1:]:
        value = value + term.astype(F32)
    return value.astype(BF)


def add_cores(coords, mine, theirs, right, left, far, own):
    rows = own.shape[0]
    for out, offset in ((right, 1), (left, 3), (far, 2), (own, 0)):
        part = block_rows(coords[0], offset, rows)
        out[...] = total(mine[part, :], theirs[part, :])


def add_x(coords, own, from_left, from_right, from_far, scratch, right, left, far, mine):
    scratch[...] = total(own[...], from_left[...], from_right[...], from_far[...])
    for out, offset in ((right, 1), (left, 3), (far, 2), (mine, 0)):
        out[...] = scratch[block_rows(coords[2], offset, out.shape[0]), :]


def add_all(coords, *refs):
    refs[-1][...] = total(*(ref[...] for ref in refs[:-1]))


def join_y(coords, own, left, right, far, out):
    for piece, offset in ((own, 0), (left, 3), (right, 1), (far, 2)):
        out[block_rows(coords[2], offset, piece.shape[0]), :] = piece[...]


def join_cores(factor, coords, own, theirs, share_in, share_out):
    core = coords[1]
    cut = share_in.shape[1] // 2
    side = share_out.shape[1] // 2

    def put(half, piece):
        share_in[:, half * cut : (half + 1) * cut] = piece[:, :cut].astype(F32) * factor
        share_out[:, half * side : (half + 1) * side] = piece[:, cut:].astype(F32) * factor

    for half in range(2):
        pl.when(core == half)(functools.partial(put, half, own))
        pl.when(core != half)(functools.partial(put, half, theirs))


def per_device(
    embedded, grad_out, w_in, w_out, lengths, slot_of, local_rows, send_counts, send_offsets
):
    fsdp_count = lax.axis_size("fsdp")
    table_count = lax.axis_size("table")
    fsdp, table = lax.axis_index("fsdp"), lax.axis_index("table")
    core = lax.rem(table, 2)
    coords = jnp.stack([fsdp, core, table // 8, lax.rem(table // 2, 4)]).astype(jnp.int32)
    counts, offsets = send_counts[0], send_offsets[0]

    def along_x(array, shift):
        return ring(array, "fsdp", 4, shift)

    def along_y(array, shift):
        return table_ring(array, 8, 4, shift, table_count)

    def along_z(array, shift):
        return table_ring(array, 2, 4, shift, table_count)

    def three_ways(along, right, left, far):
        return along(right, 1), along(left, -1), along(far, 2)

    half = jnp.concatenate(
        [lax.dynamic_slice_in_dim(a, core * 64, 64, 0) for a in (w_in, w_out)], axis=1
    )
    low, high = along_x(half, 1), along_x(half, -1)
    labels = run_labels(counts, offsets, local_rows)
    given = run_norm(embedded, labels, 0)
    low, high, *given = lax.optimization_barrier((low, high, *given))
    far_a, far_b = along_x(low[:32], 1), along_x(high[32:], -1)
    low_o, high_o = swap(low, 1, table_count), swap(high, 1, table_count)
    normed, turned = run_norm(embedded, labels, 1, given)
    far_a, far_b, normed, turned = lax.optimization_barrier((far_a, far_b, normed, turned))
    far_ao, far_bo = swap(far_a, 1, table_count), swap(far_b, 1, table_count)
    pieces = [w_in, w_out, low, high, low_o, high_o, far_a, far_b, far_ao, far_bo]

    shift = jnp.where(
        slot_of[None, :] >= offsets[1:, None], CAP - counts[:-1, None], 0
    ).sum(axis=0)
    bucket = (slot_of + shift).reshape(1, -1)

    grad_proj, tokens, gwout = run_layer(
        coords, lengths, normed, embedded, grad_out, pieces
    )
    bucket_rows = run_buckets(bucket, labels, tokens, fsdp_count)
    values = bucket_rows.reshape(fsdp_count * table_count, PACKET, 128)
    got = lax.all_to_all(values, BOTH, split_axis=0, concat_axis=0, tiled=True)

    mine, other = run_weights(coords, turned, grad_proj, gwout, bucket_rows)
    rows, cols = mine.shape
    block, part = rows // 4, rows // 16
    right, left, far, own = small_kernel(
        add_cores,
        "add_cores",
        coords,
        (mine, swap(other, 1, table_count)),
        [((block, cols), BF)] * 4,
    )
    from_x = three_ways(along_x, right, left, far)
    *tables, token = run_scatter(got, 0, 32)
    _, right, left, far, own = small_kernel(
        add_x,
        "add_x",
        coords,
        (own, *from_x),
        [((block, cols), BF)] + [((part, cols), BF)] * 4,
        after=(token,),
    )
    one = [((part, cols), BF)]
    from_y = three_ways(along_y, right, left, far)
    *tables, token = run_scatter(got, 32, 32, tables, own)
    (own,) = small_kernel(add_all, "add_y", coords, (own, *from_y), one, after=(token,))
    from_z = three_ways(along_z, own, own, own)
    *tables, token = run_scatter(got, 64, 32, tables, own)
    (own,) = small_kernel(add_all, "add_z", coords, (own, *from_z), one, after=(token,))
    from_y = three_ways(along_y, own, own, own)
    *tables, token = run_scatter(got, 96, 16, tables, own)
    (own,) = small_kernel(
        join_y, "join_y", coords, (own, *from_y), [((block, cols), BF)], after=(token,)
    )
    theirs = swap(own, 1, table_count)
    grad_table, token = run_scatter(got, 112, 16, tables, own)
    factor = 1.0 / math.sqrt(embedded.shape[0] * fsdp_count * table_count)
    share_in, share_out = small_kernel(
        functools.partial(join_cores, factor),
        "join_cores",
        coords,
        (own, theirs),
        [((block, 4 * WIDTH), F32), ((block, WIDTH), F32)],
        after=(token,),
    )
    return (share_in, share_out, grad_table)


def solution(mesh):
    placed = (
        P(BOTH, None),
        P(BOTH, None),
        P("fsdp", None),
        P("fsdp", None),
        P(BOTH),
        P(BOTH),
        P(BOTH),
        P(BOTH, None),
        P(BOTH, None),
    )
    return jax.shard_map(
        per_device,
        mesh=mesh,
        in_specs=placed,
        out_specs=(P("fsdp", None), P("fsdp", None), P("table", "fsdp")),
        check_vma=False,
    )
```

```python
import functools
import math

import jax
import jax.numpy as jnp
from jax import lax
from jax.experimental import pallas as pl
from jax.experimental.pallas import tpu as pltpu
from jax.sharding import PartitionSpec as P

HEAD_DIM = 128
ROWS_DEV = 4096
CAP = 64
PACKET = 72
SEQ = 512
WIDTH = 512
HEADS = WIDTH // HEAD_DIM
HALF = SEQ // 2
EPS = 1e-05
BF = jnp.bfloat16
F32 = jnp.float32
BOTH = ("fsdp", "table")


def dot_nn(a, b):
    return lax.dot_general(a, b, (((1,), (0,)), ((), ())), preferred_element_type=F32)


def dot_nt(a, b):
    return lax.dot_general(a, b, (((1,), (1,)), ((), ())), preferred_element_type=F32)


def dot_tn(a, b):
    return lax.dot_general(a, b, (((0,), (0,)), ((), ())), preferred_element_type=F32)


def normalise(x):
    center = x - jnp.mean(x, axis=-1, keepdims=True)
    rstd = lax.rsqrt(jnp.mean(center * center, axis=-1, keepdims=True) + EPS)
    return center * rstd, rstd


def norm_back(xhat, rstd, cot):
    return rstd * (
        cot
        - jnp.mean(cot, axis=-1, keepdims=True)
        - xhat * jnp.mean(cot * xhat, axis=-1, keepdims=True)
    )


def norm_kernel(emb, *refs):
    normed, turned = refs[-2:]
    xhat, _ = normalise(emb[...].astype(F32))
    normed[...] = xhat.astype(BF)
    turned[...] = normed[...].T


def run_norm(embedded, after, half, given=()):
    tokens = embedded.shape[0]
    steps = tokens // SEQ // 2
    first = half * steps
    anywhere = pl.BlockSpec(memory_space=pl.ANY)
    return pl.pallas_call(
        norm_kernel,
        grid=(steps,),
        in_specs=[pl.BlockSpec((SEQ, WIDTH), lambda i: (i + first, 0)), anywhere]
        + [anywhere] * len(given),
        out_specs=[
            pl.BlockSpec((SEQ, WIDTH), lambda i: (i + first, 0)),
            pl.BlockSpec((WIDTH, SEQ), lambda i: (0, i + first)),
        ],
        out_shape=[
            jax.ShapeDtypeStruct((tokens, WIDTH), BF),
            jax.ShapeDtypeStruct((WIDTH, tokens), BF),
        ],
        input_output_aliases={2 + i: i for i in range(len(given))},
        compiler_params=pltpu.CompilerParams(vmem_limit_bytes=56 * 1024 * 1024),
        cost_estimate=pl.CostEstimate(
            flops=10_000_000, bytes_accessed=3_000_000, transcendentals=1024
        ),
        name="norm",
    )(embedded, after, *given)


def layer_kernel(
    coords, lens, normed, go, emb, own_in, own_out,
    low, high, low_o, high_o, far_a, far_b, far_ao, far_bo,
    gp, tokens, gwout,
    w, w_turned, slope, hidden, probs, rates, mixed, cot, seq_sum,
):
    step = pl.program_id(0)

    @pl.when(step == 0)
    def _():
        me, core = coords[0], coords[1]

        def put(shard, which, offset, piece):
            row = lax.rem(shard, 4) * 128 + which * 64 + offset
            w[pl.ds(pl.multiple_of(row, 32), piece.shape[0]), :] = piece[...]

        home = pl.ds(pl.multiple_of(me * 128, 128), 128)
        w[home, 0 : 4 * WIDTH] = own_in[...]
        w[home, 4 * WIDTH :] = own_out[...]
        put(me + 3, core, 0, low)
        put(me + 3, 1 - core, 0, low_o)
        put(me + 1, core, 0, high)
        put(me + 1, 1 - core, 0, high_o)
        put(me + 2, core, 0, far_a)
        put(me + 2, core, 32, far_b)
        put(me + 2, 1 - core, 0, far_ao)
        put(me + 2, 1 - core, 32, far_bo)
        gwout[...] = jnp.zeros_like(gwout)

        @pl.loop(0, 4)
        def _(i):
            cols = pl.ds(pl.multiple_of(i * WIDTH, WIDTH), WIDTH)
            w_turned[cols, :] = w[:, cols].T

    for block in range(4):
        cols = slice(block * WIDTH, (block + 1) * WIDTH)
        half = 0.5 * dot_nn(normed[...], w[:, cols])
        t = jnp.tanh(half)
        ht = half * t
        hidden[:, cols] = (half + ht).astype(BF)
        slope[:, cols] = 0.5 * ((1.0 + half) + t * (1.0 - ht))

    factor = 0.5 / math.sqrt(HEAD_DIM)

    def head_cols(block, head):
        return slice(block * WIDTH + head * HEAD_DIM, block * WIDTH + (head + 1) * HEAD_DIM)

    causal = lax.broadcasted_iota(jnp.int32, (HALF, HALF), 1) <= lax.broadcasted_iota(
        jnp.int32, (HALF, HALF), 0
    )
    for head in range(HEADS):
        v_cols, q_cols, k_cols = (head_cols(b, head) for b in (1, 2, 3))
        for qi in range(2):
            q_rows = slice(qi * HALF, (qi + 1) * HALF)
            for ki in range(qi + 1):
                k_rows = slice(ki * HALF, (ki + 1) * HALF)
                z = factor * dot_nt(hidden[q_rows, q_cols], hidden[k_rows, k_cols])
                t = jnp.tanh(z)
                zt = z * t
                prob = z + zt
                rate = (1.0 + z) + t * (1.0 - zt)
                if qi == ki:
                    prob = jnp.where(causal, prob, 0.0)
                    rate = jnp.where(causal, rate, 0.0)
                probs[head, q_rows, k_rows] = prob.astype(BF)
                rates[head, q_rows, k_rows] = rate.astype(BF)
            seen = slice(0, (qi + 1) * HALF)
            mixed[q_rows, head_cols(0, head)] = dot_nn(
                probs[head, q_rows, seen], hidden[seen, v_cols]
            )

    keep = lax.broadcasted_iota(jnp.int32, (SEQ, 1), 0) < lens[step]
    raw = jnp.where(keep, mixed[...] * (1.0 / SEQ), 0.0)
    xhat, rstd = normalise(raw)
    gate = hidden[:, 0:WIDTH].astype(F32)
    down = dot_nt(go[...], w[:, 4 * WIDTH :]).astype(BF).astype(F32)
    seq_sum[...] = (xhat * gate).astype(BF)
    grad_gate = ((down * xhat).astype(BF).astype(F32) * slope[:, 0:WIDTH]).astype(BF)
    gp[:, 0:WIDTH] = grad_gate
    back = norm_back(xhat, rstd, down * gate)
    cot[...] = jnp.where(keep, back * (1.0 / SEQ), 0.0).astype(BF)
    gwout[...] += dot_tn(seq_sum[...], go[...])

    def finish(value, rows, cols):
        grad = (value.astype(BF).astype(F32) * slope[rows, cols]).astype(BF)
        gp[rows, cols] = grad

    top, low_half, whole = slice(0, HALF), slice(HALF, SEQ), slice(0, SEQ)
    for head in range(HEADS):
        v_cols, q_cols, k_cols = (head_cols(b, head) for b in (1, 2, 3))
        c_cols = head_cols(0, head)
        for q_rows, seen in ((top, top), (low_half, whole)):
            down = dot_nt(cot[q_rows, c_cols], hidden[seen, v_cols]).astype(BF)
            score = down * rates[head, q_rows, seen]
            rates[head, q_rows, seen] = score
            finish(factor * dot_nn(score, hidden[seen, k_cols]), q_rows, q_cols)
        for k_rows, seen in ((top, whole), (low_half, low_half)):
            finish(dot_tn(probs[head, seen, k_rows], cot[seen, c_cols]), k_rows, v_cols)
            finish(
                factor * dot_tn(rates[head, seen, k_rows], hidden[seen, q_cols]),
                k_rows,
                k_cols,
            )

    xhat, rstd = normalise(emb[...].astype(F32))
    back = norm_back(xhat, rstd, dot_nn(gp[...], w_turned[...]))
    tokens[...] = (back + go[...].astype(F32)).astype(BF)


def run_layer(coords, lengths, normed, embedded, grad_out, pieces):
    tokens = normed.shape[0]
    smem = pl.BlockSpec(memory_space=pltpu.SMEM)

    def whole(shape):
        return pl.BlockSpec(shape, lambda i: (0, 0))

    def by_seq(cols):
        return pl.BlockSpec((SEQ, cols), lambda i: (i, 0))

    return pl.pallas_call(
        layer_kernel,
        grid=(tokens // SEQ,),
        in_specs=[smem, smem] + [by_seq(WIDTH)] * 3 + [whole(p.shape) for p in pieces],
        out_specs=[by_seq(4 * WIDTH), by_seq(WIDTH), whole((WIDTH, WIDTH))],
        out_shape=[
            jax.ShapeDtypeStruct((tokens, 4 * WIDTH), BF),
            jax.ShapeDtypeStruct((tokens, WIDTH), BF),
            jax.ShapeDtypeStruct((WIDTH, WIDTH), F32),
        ],
        scratch_shapes=[
            pltpu.VMEM((WIDTH, 5 * WIDTH), BF),
            pltpu.VMEM((4 * WIDTH, WIDTH), BF),
            pltpu.VMEM((SEQ, 4 * WIDTH), F32),
            pltpu.VMEM((SEQ, 4 * WIDTH), BF),
            pltpu.VMEM((HEADS, SEQ, SEQ), BF),
            pltpu.VMEM((HEADS, SEQ, SEQ), BF),
            pltpu.VMEM((SEQ, WIDTH), F32),
            pltpu.VMEM((SEQ, WIDTH), BF),
            pltpu.VMEM((SEQ, WIDTH), BF),
        ],
        compiler_params=pltpu.CompilerParams(vmem_limit_bytes=56 * 1024 * 1024),
        cost_estimate=pl.CostEstimate(
            flops=20_000_000_000, bytes_accessed=20_000_000, transcendentals=8_000_000
        ),
        name="layer",
    )(coords, lengths, normed, grad_out, embedded, *pieces)


def weight_kernel(coords, turned, gp, gwout, after, mine, other):
    step = pl.program_id(0)
    core, half = coords[1], step // 2
    cols = pl.ds(pl.multiple_of(lax.rem(step, 2) * WIDTH, WIDTH), WIDTH)
    value = dot_nn(turned[...], gp[...]).astype(BF)

    @pl.when(half == core)
    def _():
        mine[:, cols] = value

    @pl.when(half != core)
    def _():
        other[:, cols] = value

    @pl.when(step == 0)
    def _():
        sides = gwout[...].astype(BF)
        first, second = sides[:, : WIDTH // 2], sides[:, WIDTH // 2 :]
        mine[:, 2 * WIDTH :] = jnp.where(core == 0, first, second)
        other[:, 2 * WIDTH :] = jnp.where(core == 0, second, first)


def run_weights(coords, turned, grad_proj, gwout, after):
    tokens = turned.shape[1]
    half = pl.BlockSpec((WIDTH, 5 * WIDTH // 2), lambda i: (0, 0))
    return pl.pallas_call(
        weight_kernel,
        grid=(4,),
        in_specs=[
            pl.BlockSpec(memory_space=pltpu.SMEM),
            pl.BlockSpec((WIDTH, tokens), lambda i: (0, 0)),
            pl.BlockSpec((tokens, WIDTH), lambda i: (0, i)),
            pl.BlockSpec((WIDTH, WIDTH), lambda i: (0, 0)),
            pl.BlockSpec(memory_space=pl.ANY),
        ],
        out_specs=[half, half],
        out_shape=[jax.ShapeDtypeStruct((WIDTH, 5 * WIDTH // 2), BF)] * 2,
        compiler_params=pltpu.CompilerParams(vmem_limit_bytes=56 * 1024 * 1024),
        cost_estimate=pl.CostEstimate(
            flops=4_300_000_000, bytes_accessed=13_000_000, transcendentals=0
        ),
        name="weight_grads",
    )(coords, turned, grad_proj, gwout, after)


def bucket_kernel(bucket, labels, tokens, out):
    owners = out.shape[1]
    tile, count = owners * CAP, tokens.shape[0]
    slot = lax.broadcasted_iota(jnp.int32, (tile, count), 0) + pl.program_id(0) * tile
    pick = jnp.where(slot == bucket[...], 1.0, 0.0).astype(BF)
    sums = dot_nn(pick, tokens[...]).astype(BF)
    upper = lax.shift_right_logical(labels[...], 6)
    lower = jnp.bitwise_and(labels[...], 63)
    lane = lax.broadcasted_iota(jnp.int32, labels.shape, 1)
    marks = jnp.where(lane < CAP, upper, pltpu.roll(lower, CAP, 1)).astype(F32).astype(BF)
    for part in range(out.shape[0]):
        for owner in range(owners):
            cols = slice(part * 128, (part + 1) * 128)
            out[part, owner, 0:CAP, :] = sums[owner * CAP : (owner + 1) * CAP, cols]
            out[part, owner, CAP:PACKET, :] = jnp.broadcast_to(
                marks[owner : owner + 1, :], (PACKET - CAP, 128)
            )


def run_buckets(bucket, labels, tokens, parts):
    count, width = tokens.shape
    owners = labels.shape[0]
    per_step = 8
    return pl.pallas_call(
        bucket_kernel,
        grid=(owners // per_step,),
        in_specs=[
            pl.BlockSpec((1, count), lambda i: (0, 0)),
            pl.BlockSpec((per_step, 128), lambda i: (i, 0)),
            pl.BlockSpec((count, width), lambda i: (0, 0)),
        ],
        out_specs=pl.BlockSpec((parts, per_step, PACKET, 128), lambda i: (0, i, 0, 0)),
        out_shape=jax.ShapeDtypeStruct((parts, owners, PACKET, 128), BF),
        compiler_params=pltpu.CompilerParams(vmem_limit_bytes=56 * 1024 * 1024),
        cost_estimate=pl.CostEstimate(
            flops=200_000_000, bytes_accessed=1_000_000, transcendentals=0
        ),
        name="bucket_rows",
    )(bucket, labels, tokens)


def label_kernel(counts, offsets, rows, out):
    lane = lax.broadcasted_iota(jnp.int32, (8, 128), 1)
    for owner in range(out.shape[0]):
        count, first = counts[owner], offsets[owner]
        start = lax.rem(first, 128)
        near = pltpu.roll(rows[pl.ds(first // 128, 8), :], lax.rem(128 - start, 128), 1)
        taken = jnp.where(lane[0:1] < 128 - start, near[0:1], near[1:2])
        out[owner : owner + 1, :] = jnp.where(lane[0:1] < count, taken, ROWS_DEV)


def run_labels(counts, offsets, rows):
    smem = pl.BlockSpec(memory_space=pltpu.SMEM)
    whole = pl.BlockSpec(memory_space=pltpu.VMEM)
    lines = -(-rows.shape[0] // 128) + 8
    rows = jnp.pad(rows, (0, lines * 128 - rows.shape[0])).reshape(lines, 128)
    return pl.pallas_call(
        label_kernel,
        in_specs=[smem, smem, whole],
        out_specs=whole,
        out_shape=jax.ShapeDtypeStruct((counts.shape[0], 2 * CAP), jnp.int32),
        cost_estimate=pl.CostEstimate(flops=10_000, bytes_accessed=10_000, transcendentals=0),
        name="labels",
    )(counts, offsets, rows)


def scatter_kernel(first, last, rows, *refs):
    if first:
        even_in, odd_in, _, *refs = refs
    if last:
        out, token, even, odd, even_block, odd_block, words, labels, sem = refs
    else:
        even, odd, token, even_block, odd_block, words, labels, sem = refs
    batch = 16
    marks = rows[:, CAP, :].astype(F32)
    marks = marks * 64.0 + pltpu.roll(marks, CAP, 1)
    words[...] = marks.astype(jnp.int32)
    copy = pltpu.make_async_copy(words, labels, sem)
    copy.start()
    if first:
        even[...] = even_in[...]
        odd[...] = odd_in[...]
    else:
        even[...] = jnp.zeros_like(even)
        odd[...] = jnp.zeros_like(odd)
    copy.wait()

    @pl.loop(0, rows.shape[0] // 2)
    def _(pair):
        both = ((2 * pair, even, even_block), (2 * pair + 1, odd, odd_block))
        for source, _, block in both:
            block[...] = rows[source, 0:CAP, :].astype(F32)

        def add_batch(start):
            todo = []
            for source, table, block in both:
                for place in range(start, start + batch):
                    here = pl.ds(labels[source, place], 1)
                    todo.append((table, here, table[here, :] + block[place : place + 1, :]))
            for table, here, value in todo:
                table[here, :] = value

        for start in range(0, CAP, batch):
            used = jnp.minimum(labels[2 * pair, start], labels[2 * pair + 1, start])
            pl.when(used != ROWS_DEV)(functools.partial(add_batch, start))

    if last:
        out[...] = even[0:ROWS_DEV, :] + odd[0:ROWS_DEV, :]
    token[...] = jnp.zeros_like(token)


def run_scatter(rows, start, count, tables=None, after=None):
    sources, packet, width = rows.shape
    first, last = start > 0, start + count == sources
    whole = pl.BlockSpec(memory_space=pltpu.VMEM)
    table = jax.ShapeDtypeStruct((ROWS_DEV + 8, width), F32)
    scratch = [
        pltpu.VMEM((CAP, width), F32),
        pltpu.VMEM((CAP, width), F32),
        pltpu.VMEM((count, 2 * CAP), jnp.int32),
        pltpu.SMEM((count, 2 * CAP), jnp.int32),
        pltpu.SemaphoreType.DMA,
    ]
    if last:
        out_shape = [jax.ShapeDtypeStruct((ROWS_DEV, width), F32)]
        scratch = [pltpu.VMEM(table.shape, F32), pltpu.VMEM(table.shape, F32)] + scratch
    else:
        out_shape = [table, table]
    out_shape.append(jax.ShapeDtypeStruct((8, 128), F32))
    return pl.pallas_call(
        functools.partial(scatter_kernel, first, last),
        grid=(1,),
        in_specs=[pl.BlockSpec((count, packet, width), lambda i: (start // count, 0, 0))]
        + ([whole, whole, pl.BlockSpec(memory_space=pl.ANY)] if first else []),
        out_specs=[whole] * len(out_shape),
        out_shape=out_shape,
        scratch_shapes=scratch,
        compiler_params=pltpu.CompilerParams(vmem_limit_bytes=24 * 1024 * 1024),
        cost_estimate=pl.CostEstimate(
            flops=2_000_000, bytes_accessed=6_000_000, transcendentals=0
        ),
        name="scatter",
    )(rows, *((*tables, after) if first else ()))


def ring(array, axis, size, shift):
    return lax.ppermute(array, axis, [(i, (i + shift) % size) for i in range(size)])


def table_ring(array, stride, size, shift, count):
    pairs = []
    for i in range(count):
        place = (i // stride) % size
        pairs.append((i, i + (((place + shift) % size) - place) * stride))
    return lax.ppermute(array, "table", pairs)


def swap(array, bit, count):
    return lax.ppermute(array, "table", [(i, i ^ bit) for i in range(count)])


def small_kernel(body, name, coords, arrays, outs, after=(), through=(), limit=16):
    def kernel(place, *refs):
        first = len(arrays) + len(after) + len(through)
        body(place, *refs[: len(arrays)], *refs[first : first + len(outs)])

    whole = pl.BlockSpec(memory_space=pltpu.VMEM)
    return pl.pallas_call(
        kernel,
        in_specs=[pl.BlockSpec(memory_space=pltpu.SMEM)]
        + [whole] * len(arrays)
        + [pl.BlockSpec(memory_space=pl.ANY)] * (len(after) + len(through)),
        out_specs=[whole] * len(outs) + [pl.BlockSpec(memory_space=pl.ANY)] * len(through),
        out_shape=[jax.ShapeDtypeStruct(shape, kind) for shape, kind in outs]
        + [jax.ShapeDtypeStruct(a.shape, a.dtype) for a in through],
        input_output_aliases={
            1 + len(arrays) + len(after) + i: len(outs) + i for i in range(len(through))
        },
        compiler_params=pltpu.CompilerParams(vmem_limit_bytes=limit * 1024 * 1024),
        cost_estimate=pl.CostEstimate(
            flops=1_000_000, bytes_accessed=2_000_000, transcendentals=0
        ),
        name=name,
    )(coords, *arrays, *after, *through)


def block_rows(place, offset, rows):
    return pl.ds(pl.multiple_of(lax.rem(place + offset, 4) * rows, rows), rows)


def total(*terms):
    value = terms[0].astype(F32)
    for term in terms[1:]:
        value = value + term.astype(F32)
    return value.astype(BF)


def add_cores(coords, mine, theirs, right, left, far, own):
    rows = own.shape[0]
    for out, offset in ((right, 1), (left, 3), (far, 2), (own, 0)):
        part = block_rows(coords[0], offset, rows)
        out[...] = total(mine[part, :], theirs[part, :])


def add_x(coords, own, from_left, from_right, from_far, right, left, far, mine):
    for out, offset in ((right, 1), (left, 3), (far, 2), (mine, 0)):
        rows = block_rows(coords[2], offset, out.shape[0])
        out[...] = total(own[rows, :], from_left[rows, :], from_right[rows, :], from_far[rows, :])


def add_all(coords, *refs):
    refs[-1][...] = total(*(ref[...] for ref in refs[:-1]))


def join_y(coords, own, left, right, far, out):
    for piece, offset in ((own, 0), (left, 3), (right, 1), (far, 2)):
        out[block_rows(coords[2], offset, piece.shape[0]), :] = piece[...]


def join_cores(factor, coords, own, theirs, share_in, share_out):
    core = coords[1]
    cut = share_in.shape[1] // 2
    side = share_out.shape[1] // 2

    def put(half, piece):
        share_in[:, half * cut : (half + 1) * cut] = piece[:, :cut].astype(F32) * factor
        share_out[:, half * side : (half + 1) * side] = piece[:, cut:].astype(F32) * factor

    for half in range(2):
        pl.when(core == half)(functools.partial(put, half, own))
        pl.when(core != half)(functools.partial(put, half, theirs))


def per_device(
    embedded, grad_out, w_in, w_out, lengths, slot_of, local_rows, send_counts, send_offsets
):
    fsdp_count = lax.axis_size("fsdp")
    table_count = lax.axis_size("table")
    fsdp, table = lax.axis_index("fsdp"), lax.axis_index("table")
    core = lax.rem(table, 2)
    coords = jnp.stack([fsdp, core, table // 8, lax.rem(table // 2, 4)]).astype(jnp.int32)
    counts, offsets = send_counts[0], send_offsets[0]

    def along_x(array, shift):
        return ring(array, "fsdp", 4, shift)

    def along_y(array, shift):
        return table_ring(array, 8, 4, shift, table_count)

    def along_z(array, shift):
        return table_ring(array, 2, 4, shift, table_count)

    def three_ways(along, right, left, far):
        return along(right, 1), along(left, -1), along(far, 2)

    half = jnp.concatenate(
        [lax.dynamic_slice_in_dim(a, core * 64, 64, 0) for a in (w_in, w_out)], axis=1
    )
    low, high = along_x(half, 1), along_x(half, -1)
    labels = run_labels(counts, offsets, local_rows)
    given = run_norm(embedded, labels, 0)
    low, high, *given = lax.optimization_barrier((low, high, *given))
    far_a, far_b = along_x(low[:32], 1), along_x(high[32:], -1)
    low_o, high_o = swap(low, 1, table_count), swap(high, 1, table_count)
    shift = jnp.where(
        slot_of[None, :] >= offsets[1:, None], CAP - counts[:-1, None], 0
    ).sum(axis=0)
    bucket = (slot_of + shift).reshape(1, -1)
    normed, turned = run_norm(embedded, labels, 1, given)
    far_a, far_b, normed, turned, coords, bucket = lax.optimization_barrier(
        (far_a, far_b, normed, turned, coords, bucket)
    )
    far_ao, far_bo = swap(far_a, 1, table_count), swap(far_b, 1, table_count)
    pieces = [w_in, w_out, low, high, low_o, high_o, far_a, far_b, far_ao, far_bo]

    grad_proj, tokens, gwout = run_layer(
        coords, lengths, normed, embedded, grad_out, pieces
    )
    bucket_rows = run_buckets(bucket, labels, tokens, fsdp_count)
    values = bucket_rows.reshape(fsdp_count * table_count, PACKET, 128)
    got = lax.all_to_all(values, BOTH, split_axis=0, concat_axis=0, tiled=True)

    mine, other = run_weights(coords, turned, grad_proj, gwout, bucket_rows)
    rows, cols = mine.shape
    block, part = rows // 4, rows // 16
    right, left, far, own = small_kernel(
        add_cores,
        "add_cores",
        coords,
        (mine, swap(other, 1, table_count)),
        [((block, cols), BF)] * 4,
    )
    from_x = three_ways(along_x, right, left, far)
    *tables, token = run_scatter(got, 0, 96)
    right, left, far, own = small_kernel(
        add_x,
        "add_x",
        coords,
        (own, *from_x),
        [((part, cols), BF)] * 4,
        after=(token,),
    )
    one = [((part, cols), BF)]
    from_y = three_ways(along_y, right, left, far)
    (own,) = small_kernel(add_all, "add_y", coords, (own, *from_y), one)
    from_z = three_ways(along_z, own, own, own)
    *tables, token = run_scatter(got, 96, 16, tables, own)
    (own,) = small_kernel(add_all, "add_z", coords, (own, *from_z), one, after=(token,))
    from_y = three_ways(along_y, own, own, own)
    grad_table, token = run_scatter(got, 112, 16, tables, own)
    (own,) = small_kernel(
        join_y, "join_y", coords, (own, *from_y), [((block, cols), BF)], after=(token,)
    )
    theirs = swap(own, 1, table_count)
    factor = 1.0 / math.sqrt(embedded.shape[0] * fsdp_count * table_count)
    share_in, share_out = small_kernel(
        functools.partial(join_cores, factor),
        "join_cores",
        coords,
        (own, theirs),
        [((block, 4 * WIDTH), F32), ((block, WIDTH), F32)],
    )
    return (share_in, share_out, grad_table)


def solution(mesh):
    placed = (
        P(BOTH, None),
        P(BOTH, None),
        P("fsdp", None),
        P("fsdp", None),
        P(BOTH),
        P(BOTH),
        P(BOTH),
        P(BOTH, None),
        P(BOTH, None),
    )
    return jax.shard_map(
        per_device,
        mesh=mesh,
        in_specs=placed,
        out_specs=(P("fsdp", None), P("fsdp", None), P("table", "fsdp")),
        check_vma=False,
    )
```

```python
import functools
import math

import jax
import jax.numpy as jnp
from jax import lax
from jax.experimental import pallas as pl
from jax.experimental.pallas import tpu as pltpu
from jax.sharding import PartitionSpec as P

HEAD_DIM = 128
ROWS_DEV = 4096
CAP = 64
PACKET = 72
SEQ = 512
WIDTH = 512
HEADS = WIDTH // HEAD_DIM
HALF = SEQ // 2
EPS = 1e-05
BF = jnp.bfloat16
F32 = jnp.float32
BOTH = ("fsdp", "table")


def dot_nn(a, b):
    return lax.dot_general(a, b, (((1,), (0,)), ((), ())), preferred_element_type=F32)


def dot_nt(a, b):
    return lax.dot_general(a, b, (((1,), (1,)), ((), ())), preferred_element_type=F32)


def dot_tn(a, b):
    return lax.dot_general(a, b, (((0,), (0,)), ((), ())), preferred_element_type=F32)


def normalise(x):
    center = x - jnp.mean(x, axis=-1, keepdims=True)
    rstd = lax.rsqrt(jnp.mean(center * center, axis=-1, keepdims=True) + EPS)
    return center * rstd, rstd


def norm_back(xhat, rstd, cot):
    return rstd * (
        cot
        - jnp.mean(cot, axis=-1, keepdims=True)
        - xhat * jnp.mean(cot * xhat, axis=-1, keepdims=True)
    )


def norm_kernel(emb, *refs):
    normed, turned = refs[-2:]
    xhat, _ = normalise(emb[...].astype(F32))
    normed[...] = xhat.astype(BF)
    turned[...] = normed[...].T


def run_norm(embedded, after, half, given=()):
    tokens = embedded.shape[0]
    steps = tokens // SEQ // 2
    first = half * steps
    anywhere = pl.BlockSpec(memory_space=pl.ANY)
    return pl.pallas_call(
        norm_kernel,
        grid=(steps,),
        in_specs=[pl.BlockSpec((SEQ, WIDTH), lambda i: (i + first, 0)), anywhere]
        + [anywhere] * len(given),
        out_specs=[
            pl.BlockSpec((SEQ, WIDTH), lambda i: (i + first, 0)),
            pl.BlockSpec((WIDTH, SEQ), lambda i: (0, i + first)),
        ],
        out_shape=[
            jax.ShapeDtypeStruct((tokens, WIDTH), BF),
            jax.ShapeDtypeStruct((WIDTH, tokens), BF),
        ],
        input_output_aliases={2 + i: i for i in range(len(given))},
        compiler_params=pltpu.CompilerParams(vmem_limit_bytes=56 * 1024 * 1024),
        cost_estimate=pl.CostEstimate(
            flops=10_000_000, bytes_accessed=3_000_000, transcendentals=1024
        ),
        name="norm",
    )(embedded, after, *given)


def fill_packets(bucket, labels, tokens, packets):
    parts, owners, _, width = packets.shape
    group = 8
    tile, count = group * CAP, tokens.shape[0]

    @pl.loop(0, owners // group)
    def _(i):
        slot = lax.broadcasted_iota(jnp.int32, (tile, count), 0) + i * tile
        pick = jnp.where(slot == bucket[...], 1.0, 0.0).astype(BF)
        sums = dot_nn(pick, tokens[...]).astype(BF)
        numbers = labels[pl.ds(pl.multiple_of(i * group, group), group), :]
        upper = lax.shift_right_logical(numbers, 6)
        lower = pltpu.roll(jnp.bitwise_and(numbers, 63), CAP, 1)
        lane = lax.broadcasted_iota(jnp.int32, numbers.shape, 1)
        marks = jnp.where(lane < CAP, upper, lower).astype(F32).astype(BF)
        for part in range(parts):
            cols = slice(part * width, (part + 1) * width)
            for owner in range(group):
                place = i * group + owner
                packets[part, place, 0:CAP, :] = sums[owner * CAP : (owner + 1) * CAP, cols]
                packets[part, place, CAP:PACKET, :] = jnp.broadcast_to(
                    marks[owner : owner + 1, :], (PACKET - CAP, width)
                )


def layer_kernel(
    coords, lens, bucket, labels, normed, go, emb, own_in, own_out,
    low, high, low_o, high_o, far_a, far_b, far_ao, far_bo,
    gp, gwout, packets,
    w, w_turned, tokens, slope, hidden, probs, rates, mixed, cot, seq_sum,
):
    step = pl.program_id(0)

    @pl.when(step == 0)
    def _():
        me, core = coords[0], coords[1]

        def put(shard, which, offset, piece):
            row = lax.rem(shard, 4) * 128 + which * 64 + offset
            w[pl.ds(pl.multiple_of(row, 32), piece.shape[0]), :] = piece[...]

        home = pl.ds(pl.multiple_of(me * 128, 128), 128)
        w[home, 0 : 4 * WIDTH] = own_in[...]
        w[home, 4 * WIDTH :] = own_out[...]
        put(me + 3, core, 0, low)
        put(me + 3, 1 - core, 0, low_o)
        put(me + 1, core, 0, high)
        put(me + 1, 1 - core, 0, high_o)
        put(me + 2, core, 0, far_a)
        put(me + 2, core, 32, far_b)
        put(me + 2, 1 - core, 0, far_ao)
        put(me + 2, 1 - core, 32, far_bo)
        gwout[...] = jnp.zeros_like(gwout)

        @pl.loop(0, 4)
        def _(i):
            cols = pl.ds(pl.multiple_of(i * WIDTH, WIDTH), WIDTH)
            w_turned[cols, :] = w[:, cols].T

    for block in range(4):
        cols = slice(block * WIDTH, (block + 1) * WIDTH)
        half = 0.5 * dot_nn(normed[...], w[:, cols])
        t = jnp.tanh(half)
        ht = half * t
        hidden[:, cols] = (half + ht).astype(BF)
        slope[:, cols] = 0.5 * ((1.0 + half) + t * (1.0 - ht))

    factor = 0.5 / math.sqrt(HEAD_DIM)

    def head_cols(block, head):
        return slice(block * WIDTH + head * HEAD_DIM, block * WIDTH + (head + 1) * HEAD_DIM)

    causal = lax.broadcasted_iota(jnp.int32, (HALF, HALF), 1) <= lax.broadcasted_iota(
        jnp.int32, (HALF, HALF), 0
    )
    for head in range(HEADS):
        v_cols, q_cols, k_cols = (head_cols(b, head) for b in (1, 2, 3))
        for qi in range(2):
            q_rows = slice(qi * HALF, (qi + 1) * HALF)
            for ki in range(qi + 1):
                k_rows = slice(ki * HALF, (ki + 1) * HALF)
                z = factor * dot_nt(hidden[q_rows, q_cols], hidden[k_rows, k_cols])
                t = jnp.tanh(z)
                zt = z * t
                prob = z + zt
                rate = (1.0 + z) + t * (1.0 - zt)
                if qi == ki:
                    prob = jnp.where(causal, prob, 0.0)
                    rate = jnp.where(causal, rate, 0.0)
                probs[head, q_rows, k_rows] = prob.astype(BF)
                rates[head, q_rows, k_rows] = rate.astype(BF)
            seen = slice(0, (qi + 1) * HALF)
            mixed[q_rows, head_cols(0, head)] = dot_nn(
                probs[head, q_rows, seen], hidden[seen, v_cols]
            )

    keep = lax.broadcasted_iota(jnp.int32, (SEQ, 1), 0) < lens[step]
    raw = jnp.where(keep, mixed[...] * (1.0 / SEQ), 0.0)
    xhat, rstd = normalise(raw)
    gate = hidden[:, 0:WIDTH].astype(F32)
    down = dot_nt(go[...], w[:, 4 * WIDTH :]).astype(BF).astype(F32)
    seq_sum[...] = (xhat * gate).astype(BF)
    grad_gate = ((down * xhat).astype(BF).astype(F32) * slope[:, 0:WIDTH]).astype(BF)
    gp[:, 0:WIDTH] = grad_gate
    back = norm_back(xhat, rstd, down * gate)
    cot[...] = jnp.where(keep, back * (1.0 / SEQ), 0.0).astype(BF)
    gwout[...] += dot_tn(seq_sum[...], go[...])

    def finish(value, rows, cols):
        grad = (value.astype(BF).astype(F32) * slope[rows, cols]).astype(BF)
        gp[rows, cols] = grad

    top, low_half, whole = slice(0, HALF), slice(HALF, SEQ), slice(0, SEQ)
    for head in range(HEADS):
        v_cols, q_cols, k_cols = (head_cols(b, head) for b in (1, 2, 3))
        c_cols = head_cols(0, head)
        for q_rows, seen in ((top, top), (low_half, whole)):
            down = dot_nt(cot[q_rows, c_cols], hidden[seen, v_cols]).astype(BF)
            score = down * rates[head, q_rows, seen]
            rates[head, q_rows, seen] = score
            finish(factor * dot_nn(score, hidden[seen, k_cols]), q_rows, q_cols)
        for k_rows, seen in ((top, whole), (low_half, low_half)):
            finish(dot_tn(probs[head, seen, k_rows], cot[seen, c_cols]), k_rows, v_cols)
            finish(
                factor * dot_tn(rates[head, seen, k_rows], hidden[seen, q_cols]),
                k_rows,
                k_cols,
            )

    xhat, rstd = normalise(emb[...].astype(F32))
    back = norm_back(xhat, rstd, dot_nn(gp[...], w_turned[...]))
    here = pl.ds(pl.multiple_of(step * SEQ, SEQ), SEQ)
    tokens[here, :] = (back + go[...].astype(F32)).astype(BF)

    @pl.when(step == pl.num_programs(0) - 1)
    def _():
        fill_packets(bucket, labels, tokens, packets)


def run_layer(coords, lengths, bucket, labels, normed, embedded, grad_out, pieces, parts):
    tokens = normed.shape[0]
    packets = (parts, labels.shape[0], PACKET, WIDTH // parts)
    smem = pl.BlockSpec(memory_space=pltpu.SMEM)

    def whole(shape):
        return pl.BlockSpec(shape, lambda i: (0, 0))

    def by_seq(cols):
        return pl.BlockSpec((SEQ, cols), lambda i: (i, 0))

    return pl.pallas_call(
        layer_kernel,
        grid=(tokens // SEQ,),
        in_specs=[smem, smem, whole(bucket.shape), whole(labels.shape)]
        + [by_seq(WIDTH)] * 3
        + [whole(p.shape) for p in pieces],
        out_specs=[
            by_seq(4 * WIDTH),
            whole((WIDTH, WIDTH)),
            pl.BlockSpec(packets, lambda i: (0, 0, 0, 0)),
        ],
        out_shape=[
            jax.ShapeDtypeStruct((tokens, 4 * WIDTH), BF),
            jax.ShapeDtypeStruct((WIDTH, WIDTH), F32),
            jax.ShapeDtypeStruct(packets, BF),
        ],
        scratch_shapes=[
            pltpu.VMEM((WIDTH, 5 * WIDTH), BF),
            pltpu.VMEM((4 * WIDTH, WIDTH), BF),
            pltpu.VMEM((tokens, WIDTH), BF),
            pltpu.VMEM((SEQ, 4 * WIDTH), F32),
            pltpu.VMEM((SEQ, 4 * WIDTH), BF),
            pltpu.VMEM((HEADS, SEQ, SEQ), BF),
            pltpu.VMEM((HEADS, SEQ, SEQ), BF),
            pltpu.VMEM((SEQ, WIDTH), F32),
            pltpu.VMEM((SEQ, WIDTH), BF),
            pltpu.VMEM((SEQ, WIDTH), BF),
        ],
        compiler_params=pltpu.CompilerParams(vmem_limit_bytes=56 * 1024 * 1024),
        cost_estimate=pl.CostEstimate(
            flops=20_000_000_000, bytes_accessed=20_000_000, transcendentals=8_000_000
        ),
        name="layer",
    )(coords, lengths, bucket, labels, normed, grad_out, embedded, *pieces)


def weight_kernel(coords, turned, gp, gwout, after, mine, other):
    step = pl.program_id(0)
    core, half = coords[1], step // 2
    cols = pl.ds(pl.multiple_of(lax.rem(step, 2) * WIDTH, WIDTH), WIDTH)
    value = dot_nn(turned[...], gp[...]).astype(BF)

    @pl.when(half == core)
    def _():
        mine[:, cols] = value

    @pl.when(half != core)
    def _():
        other[:, cols] = value

    @pl.when(step == 0)
    def _():
        sides = gwout[...].astype(BF)
        first, second = sides[:, : WIDTH // 2], sides[:, WIDTH // 2 :]
        mine[:, 2 * WIDTH :] = jnp.where(core == 0, first, second)
        other[:, 2 * WIDTH :] = jnp.where(core == 0, second, first)


def run_weights(coords, turned, grad_proj, gwout, after):
    tokens = turned.shape[1]
    half = pl.BlockSpec((WIDTH, 5 * WIDTH // 2), lambda i: (0, 0))
    return pl.pallas_call(
        weight_kernel,
        grid=(4,),
        in_specs=[
            pl.BlockSpec(memory_space=pltpu.SMEM),
            pl.BlockSpec((WIDTH, tokens), lambda i: (0, 0)),
            pl.BlockSpec((tokens, WIDTH), lambda i: (0, i)),
            pl.BlockSpec((WIDTH, WIDTH), lambda i: (0, 0)),
            pl.BlockSpec(memory_space=pl.ANY),
        ],
        out_specs=[half, half],
        out_shape=[jax.ShapeDtypeStruct((WIDTH, 5 * WIDTH // 2), BF)] * 2,
        compiler_params=pltpu.CompilerParams(vmem_limit_bytes=56 * 1024 * 1024),
        cost_estimate=pl.CostEstimate(
            flops=4_300_000_000, bytes_accessed=13_000_000, transcendentals=0
        ),
        name="weight_grads",
    )(coords, turned, grad_proj, gwout, after)


def label_kernel(counts, offsets, rows, out):
    lane = lax.broadcasted_iota(jnp.int32, (8, 128), 1)
    for owner in range(out.shape[0]):
        count, first = counts[owner], offsets[owner]
        start = lax.rem(first, 128)
        near = pltpu.roll(rows[pl.ds(first // 128, 8), :], lax.rem(128 - start, 128), 1)
        taken = jnp.where(lane[0:1] < 128 - start, near[0:1], near[1:2])
        out[owner : owner + 1, :] = jnp.where(lane[0:1] < count, taken, ROWS_DEV)


def run_labels(counts, offsets, rows):
    smem = pl.BlockSpec(memory_space=pltpu.SMEM)
    whole = pl.BlockSpec(memory_space=pltpu.VMEM)
    lines = -(-rows.shape[0] // 128) + 8
    rows = jnp.pad(rows, (0, lines * 128 - rows.shape[0])).reshape(lines, 128)
    return pl.pallas_call(
        label_kernel,
        in_specs=[smem, smem, whole],
        out_specs=whole,
        out_shape=jax.ShapeDtypeStruct((counts.shape[0], 2 * CAP), jnp.int32),
        cost_estimate=pl.CostEstimate(flops=10_000, bytes_accessed=10_000, transcendentals=0),
        name="labels",
    )(counts, offsets, rows)


def scatter_kernel(first, last, rows, *refs):
    if first:
        even_in, odd_in, _, *refs = refs
    if last:
        out, token, even, odd, even_block, odd_block, words, labels, sem = refs
    else:
        even, odd, token, even_block, odd_block, words, labels, sem = refs
    batch = 16
    marks = rows[:, CAP, :].astype(F32)
    marks = marks * 64.0 + pltpu.roll(marks, CAP, 1)
    words[...] = marks.astype(jnp.int32)
    copy = pltpu.make_async_copy(words, labels, sem)
    copy.start()
    if first:
        even[...] = even_in[...]
        odd[...] = odd_in[...]
    else:
        even[...] = jnp.zeros_like(even)
        odd[...] = jnp.zeros_like(odd)
    copy.wait()

    @pl.loop(0, rows.shape[0] // 2)
    def _(pair):
        both = ((2 * pair, even, even_block), (2 * pair + 1, odd, odd_block))
        for source, _, block in both:
            block[...] = rows[source, 0:CAP, :].astype(F32)

        def add_batch(start):
            todo = []
            for source, table, block in both:
                for place in range(start, start + batch):
                    here = pl.ds(labels[source, place], 1)
                    todo.append((table, here, table[here, :] + block[place : place + 1, :]))
            for table, here, value in todo:
                table[here, :] = value

        for start in range(0, CAP, batch):
            used = jnp.minimum(labels[2 * pair, start], labels[2 * pair + 1, start])
            pl.when(used != ROWS_DEV)(functools.partial(add_batch, start))

    if last:
        out[...] = even[0:ROWS_DEV, :] + odd[0:ROWS_DEV, :]
    token[...] = jnp.zeros_like(token)


def run_scatter(rows, start, count, tables=None, after=None):
    sources, packet, width = rows.shape
    first, last = start > 0, start + count == sources
    whole = pl.BlockSpec(memory_space=pltpu.VMEM)
    table = jax.ShapeDtypeStruct((ROWS_DEV + 8, width), F32)
    scratch = [
        pltpu.VMEM((CAP, width), F32),
        pltpu.VMEM((CAP, width), F32),
        pltpu.VMEM((count, 2 * CAP), jnp.int32),
        pltpu.SMEM((count, 2 * CAP), jnp.int32),
        pltpu.SemaphoreType.DMA,
    ]
    if last:
        out_shape = [jax.ShapeDtypeStruct((ROWS_DEV, width), F32)]
        scratch = [pltpu.VMEM(table.shape, F32), pltpu.VMEM(table.shape, F32)] + scratch
    else:
        out_shape = [table, table]
    out_shape.append(jax.ShapeDtypeStruct((8, 128), F32))
    return pl.pallas_call(
        functools.partial(scatter_kernel, first, last),
        grid=(1,),
        in_specs=[pl.BlockSpec((count, packet, width), lambda i: (start // count, 0, 0))]
        + ([whole, whole, pl.BlockSpec(memory_space=pl.ANY)] if first else []),
        out_specs=[whole] * len(out_shape),
        out_shape=out_shape,
        scratch_shapes=scratch,
        compiler_params=pltpu.CompilerParams(vmem_limit_bytes=24 * 1024 * 1024),
        cost_estimate=pl.CostEstimate(
            flops=2_000_000, bytes_accessed=6_000_000, transcendentals=0
        ),
        name="scatter",
    )(rows, *((*tables, after) if first else ()))


def ring(array, axis, size, shift):
    return lax.ppermute(array, axis, [(i, (i + shift) % size) for i in range(size)])


def table_ring(array, stride, size, shift, count):
    pairs = []
    for i in range(count):
        place = (i // stride) % size
        pairs.append((i, i + (((place + shift) % size) - place) * stride))
    return lax.ppermute(array, "table", pairs)


def swap(array, bit, count):
    return lax.ppermute(array, "table", [(i, i ^ bit) for i in range(count)])


def small_kernel(body, name, coords, arrays, outs, after=(), through=(), limit=16):
    def kernel(place, *refs):
        first = len(arrays) + len(after) + len(through)
        body(place, *refs[: len(arrays)], *refs[first : first + len(outs)])

    whole = pl.BlockSpec(memory_space=pltpu.VMEM)
    return pl.pallas_call(
        kernel,
        in_specs=[pl.BlockSpec(memory_space=pltpu.SMEM)]
        + [whole] * len(arrays)
        + [pl.BlockSpec(memory_space=pl.ANY)] * (len(after) + len(through)),
        out_specs=[whole] * len(outs) + [pl.BlockSpec(memory_space=pl.ANY)] * len(through),
        out_shape=[jax.ShapeDtypeStruct(shape, kind) for shape, kind in outs]
        + [jax.ShapeDtypeStruct(a.shape, a.dtype) for a in through],
        input_output_aliases={
            1 + len(arrays) + len(after) + i: len(outs) + i for i in range(len(through))
        },
        compiler_params=pltpu.CompilerParams(vmem_limit_bytes=limit * 1024 * 1024),
        cost_estimate=pl.CostEstimate(
            flops=1_000_000, bytes_accessed=2_000_000, transcendentals=0
        ),
        name=name,
    )(coords, *arrays, *after, *through)


def block_rows(place, offset, rows):
    return pl.ds(pl.multiple_of(lax.rem(place + offset, 4) * rows, rows), rows)


def total(*terms):
    value = terms[0].astype(F32)
    for term in terms[1:]:
        value = value + term.astype(F32)
    return value.astype(BF)


def add_cores(coords, mine, theirs, right, left, far, own):
    rows = own.shape[0]
    for out, offset in ((right, 1), (left, 3), (far, 2), (own, 0)):
        part = block_rows(coords[0], offset, rows)
        out[...] = total(mine[part, :], theirs[part, :])


def add_x(coords, own, from_left, from_right, from_far, right, left, far, mine):
    for out, offset in ((right, 1), (left, 3), (far, 2), (mine, 0)):
        rows = block_rows(coords[2], offset, out.shape[0])
        out[...] = total(own[rows, :], from_left[rows, :], from_right[rows, :], from_far[rows, :])


def add_all(coords, *refs):
    refs[-1][...] = total(*(ref[...] for ref in refs[:-1]))


def join_y(coords, own, left, right, far, out):
    for piece, offset in ((own, 0), (left, 3), (right, 1), (far, 2)):
        out[block_rows(coords[2], offset, piece.shape[0]), :] = piece[...]


def join_cores(factor, coords, own, theirs, share_in, share_out):
    core = coords[1]
    cut = share_in.shape[1] // 2
    side = share_out.shape[1] // 2

    def put(half, piece):
        share_in[:, half * cut : (half + 1) * cut] = piece[:, :cut].astype(F32) * factor
        share_out[:, half * side : (half + 1) * side] = piece[:, cut:].astype(F32) * factor

    for half in range(2):
        pl.when(core == half)(functools.partial(put, half, own))
        pl.when(core != half)(functools.partial(put, half, theirs))


def per_device(
    embedded, grad_out, w_in, w_out, lengths, slot_of, local_rows, send_counts, send_offsets
):
    fsdp_count = lax.axis_size("fsdp")
    table_count = lax.axis_size("table")
    fsdp, table = lax.axis_index("fsdp"), lax.axis_index("table")
    core = lax.rem(table, 2)
    coords = jnp.stack([fsdp, core, table // 8, lax.rem(table // 2, 4)]).astype(jnp.int32)
    counts, offsets = send_counts[0], send_offsets[0]

    def along_x(array, shift):
        return ring(array, "fsdp", 4, shift)

    def along_y(array, shift):
        return table_ring(array, 8, 4, shift, table_count)

    def along_z(array, shift):
        return table_ring(array, 2, 4, shift, table_count)

    def three_ways(along, right, left, far):
        return along(right, 1), along(left, -1), along(far, 2)

    half = jnp.concatenate(
        [lax.dynamic_slice_in_dim(a, core * 64, 64, 0) for a in (w_in, w_out)], axis=1
    )
    low, high = along_x(half, 1), along_x(half, -1)
    labels = run_labels(counts, offsets, local_rows)
    given = run_norm(embedded, labels, 0)
    low, high, *given = lax.optimization_barrier((low, high, *given))
    far_a, far_b = along_x(low[:32], 1), along_x(high[32:], -1)
    low_o, high_o = swap(low, 1, table_count), swap(high, 1, table_count)
    shift = jnp.where(
        slot_of[None, :] >= offsets[1:, None], CAP - counts[:-1, None], 0
    ).sum(axis=0)
    bucket = (slot_of + shift).reshape(1, -1)
    normed, turned = run_norm(embedded, labels, 1, given)
    far_a, far_b, normed, turned, coords, bucket = lax.optimization_barrier(
        (far_a, far_b, normed, turned, coords, bucket)
    )
    far_ao, far_bo = swap(far_a, 1, table_count), swap(far_b, 1, table_count)
    pieces = [w_in, w_out, low, high, low_o, high_o, far_a, far_b, far_ao, far_bo]

    grad_proj, gwout, bucket_rows = run_layer(
        coords, lengths, bucket, labels, normed, embedded, grad_out, pieces, fsdp_count
    )
    values = bucket_rows.reshape(fsdp_count * table_count, PACKET, 128)
    got = lax.all_to_all(values, BOTH, split_axis=0, concat_axis=0, tiled=True)

    mine, other = run_weights(coords, turned, grad_proj, gwout, bucket_rows)
    rows, cols = mine.shape
    block, part = rows // 4, rows // 16
    right, left, far, own = small_kernel(
        add_cores,
        "add_cores",
        coords,
        (mine, swap(other, 1, table_count)),
        [((block, cols), BF)] * 4,
    )
    from_x = three_ways(along_x, right, left, far)
    *tables, token = run_scatter(got, 0, 96)
    right, left, far, own = small_kernel(
        add_x,
        "add_x",
        coords,
        (own, *from_x),
        [((part, cols), BF)] * 4,
        after=(token,),
    )
    one = [((part, cols), BF)]
    from_y = three_ways(along_y, right, left, far)
    (own,) = small_kernel(add_all, "add_y", coords, (own, *from_y), one)
    from_z = three_ways(along_z, own, own, own)
    *tables, token = run_scatter(got, 96, 16, tables, own)
    (own,) = small_kernel(add_all, "add_z", coords, (own, *from_z), one, after=(token,))
    from_y = three_ways(along_y, own, own, own)
    grad_table, token = run_scatter(got, 112, 16, tables, own)
    (own,) = small_kernel(
        join_y, "join_y", coords, (own, *from_y), [((block, cols), BF)], after=(token,)
    )
    theirs = swap(own, 1, table_count)
    factor = 1.0 / math.sqrt(embedded.shape[0] * fsdp_count * table_count)
    share_in, share_out = small_kernel(
        functools.partial(join_cores, factor),
        "join_cores",
        coords,
        (own, theirs),
        [((block, 4 * WIDTH), F32), ((block, WIDTH), F32)],
    )
    return (share_in, share_out, grad_table)


def solution(mesh):
    placed = (
        P(BOTH, None),
        P(BOTH, None),
        P("fsdp", None),
        P("fsdp", None),
        P(BOTH),
        P(BOTH),
        P(BOTH),
        P(BOTH, None),
        P(BOTH, None),
    )
    return jax.shard_map(
        per_device,
        mesh=mesh,
        in_specs=placed,
        out_specs=(P("fsdp", None), P("fsdp", None), P("table", "fsdp")),
        check_vma=False,
    )
```
